256 devices in a mesh: tm: 8 (over z_lo, core), chan: 32 (over z_hi, x, y).
Axes of the slice: x: 4, y: 4, z: 8 (z_hi: 2, z_lo: 4; z = z_hi * 4 + z_lo), core: 2. Of those that a mesh axis runs over, the one named last changes fastest.
Arguments:
- strain_rate: bfloat16 [2048, 24, 16384], P('chan', 'tm'), may hold values from -600 to 600
- fir_taps: bfloat16 [32], replicated, may hold values from -1 to 1
- source_channels: int32 [128], replicated, may hold values from 0 to 2047
Outputs:
- correlations: float32 [128, 2048, 1024], P(None, ('chan', 'tm'))
The draws below stay inside these ranges and needn't reach their ends.
Inputs may be any that keep to these rules, and one draw needn't show every extreme that they name: `source_channels`: repeats may occur.
All inputs are finite; a program needn't handle non-finite values.
Results may differ from the reference program's by a relative error of at most 0.0029.
Values may be sent and summed in bfloat16 or wider, within the bound.
A program may use at most 192 MiB of HBM per device.

```python
import math
import jax
import jax.numpy as jnp
from jax import lax

CH_DEV = 64
WIN = 4096
TAPS = 32
NFREQ = 512
BANDW = 64
K_LO = 32
LAGS = 1024
SRC = 128
CH = 2048
NW = 24
N_TM = 8


def draw_strain_rate(key, part):
    key = jax.random.fold_in(key, 11)
    key_chan, key_window, key_random = jax.random.split(key, 3)
    chan_scale = 10.0 ** jax.random.uniform(key_chan, (CH, 1, 1), jnp.float32)
    window_scale = 10.0 ** jax.random.uniform(key_window, (1, NW, 1), jnp.float32)
    values = jnp.clip(jax.random.normal(key_random, (CH, NW, 4 * WIN), jnp.float32), -6.0, 6.0)
    return (values * chan_scale * window_scale).astype(jnp.bfloat16)


def plant(values, own_key, smallest, top_value):
    index_at = [jax.random.randint(jax.random.fold_in(own_key, axis), (), 0, length) for axis, length in enumerate(values.shape)]
    longest = values.shape.index(max(values.shape))
    next_to = index_at[:longest] + [(index_at[longest] + 1) % values.shape[longest]] + index_at[longest + 1:]
    return values.at[tuple(index_at)].set(smallest).at[tuple(next_to)].set(top_value)


def normal_values(rng, extent, spread, limit, kind=jnp.bfloat16):
    return jnp.clip(spread * jax.random.normal(rng, extent, jnp.float32), -limit, limit).astype(kind)


def setup_inputs(seed: int = 0) -> dict:
    key_of = jax.random.split(jax.random.key(seed), 4)
    return {
        "strain_rate": draw_strain_rate(jax.random.fold_in(key_of[3], 71), 0),
        "fir_taps": normal_values(key_of[1], (TAPS,), TAPS ** -0.5, 1.0),
        "source_channels": plant(jax.random.randint(key_of[2], (SRC,), 0, CH), jax.random.fold_in(key_of[2], 1), 0, CH - 1).astype(jnp.int32),
    }


def forward_table(length, bins, first_bin):
    sample_index = lax.broadcasted_iota(jnp.int32, (length, bins), 0)
    bin_index = lax.broadcasted_iota(jnp.int32, (length, bins), 1) + first_bin
    phases = sample_index * bin_index % (2 * length)
    angles = phases.astype(jnp.float32) * (math.pi / length)
    return jnp.concatenate([jnp.cos(angles), -jnp.sin(angles)], axis=1)

def lag_table(bins, first_bin, length, lag_count):
    bin_index = lax.broadcasted_iota(jnp.int32, (bins, lag_count), 0) + first_bin
    lag_index = lax.broadcasted_iota(jnp.int32, (bins, lag_count), 1) - lag_count // 2 + 2 * length
    phases = bin_index * lag_index % (2 * length)
    angles = phases.astype(jnp.float32) * (math.pi / length)
    return jnp.concatenate([jnp.cos(angles), -jnp.sin(angles)], axis=0)

def whiten(records, fir_taps, table, bins, band_width):
    channels, windows, samples = records.shape
    length = samples // 4
    signal = records.reshape(channels * windows, 1, samples)
    kernel = fir_taps.reshape(1, 1, -1)
    decimated = lax.conv_general_dilated(signal, kernel, (4,), [(fir_taps.shape[0] - 1, 0)], preferred_element_type=jnp.float32)
    decimated = decimated.reshape(channels * windows, length)
    spectrum = jnp.dot(decimated, table, precision=lax.Precision.HIGHEST, preferred_element_type=jnp.float32)
    grouped = spectrum.reshape(channels * windows, 2, bins // band_width, band_width)
    band_power = lax.optimization_barrier(jnp.sum(grouped * grouped, axis=(1, 3), keepdims=True)) / band_width
    whitened = grouped * lax.rsqrt(band_power + 1e-06)
    return whitened.reshape(channels, windows, 2, bins).astype(jnp.bfloat16)

def cross_spectra(source_part, local_part):
    src_real = source_part[:, :, 0].astype(jnp.float32)
    src_imag = source_part[:, :, 1].astype(jnp.float32)
    loc_real = local_part[:, :, 0].astype(jnp.float32)
    loc_imag = local_part[:, :, 1].astype(jnp.float32)
    pattern = 'swk,cwk->sck'
    highest = lax.Precision.HIGHEST
    real_part = jnp.einsum(pattern, src_real, loc_real, precision=highest) + jnp.einsum(pattern, src_imag, loc_imag, precision=highest)
    imag_part = jnp.einsum(pattern, src_imag, loc_real, precision=highest) - jnp.einsum(pattern, src_real, loc_imag, precision=highest)
    return jnp.stack([real_part, imag_part], axis=2)

def correlate(cross_spec, table, window_total):
    sources, channels, _, bins = cross_spec.shape
    flattened = cross_spec.reshape(sources * channels, 2 * bins)
    result = jnp.dot(flattened, table, precision=lax.Precision.HIGHEST, preferred_element_type=jnp.float32)
    result = result * (1.0 / math.sqrt(bins * window_total))
    return result.reshape(sources, channels, table.shape[1])

def reference(strain_rate, fir_taps, source_channels):
    ftable = forward_table(WIN, NFREQ, K_LO)
    ltable = lag_table(NFREQ, K_LO, WIN, LAGS)
    blocks = strain_rate.reshape(CH // CH_DEV, CH_DEV, NW, 4 * WIN)
    spectra = lax.map(lambda piece: whiten(piece, fir_taps, ftable, NFREQ, BANDW), blocks)
    spectra = spectra.reshape(CH, NW, 2, NFREQ)
    source_part = spectra[source_channels]
    local_rows = CH_DEV // N_TM
    pieces = spectra.reshape(CH // local_rows, local_rows, NW, 2, NFREQ)

    def one_block(piece):
        return correlate(cross_spectra(source_part, piece), ltable, NW)
    result = lax.map(one_block, pieces)
    return jnp.transpose(result, (1, 0, 2, 3)).reshape(SRC, CH, LAGS)
```

```python
import functools
import math

import jax
import jax.numpy as jnp
import ml_dtypes
import numpy as np
from jax import lax
from jax.experimental import pallas as pl
from jax.experimental.pallas import tpu as pltpu
from jax.sharding import PartitionSpec as P

WIN = 4096
NFREQ = 512
BANDW = 64
K_LO = 32
LAGS = 1024
TAPS = 32
NW = 24
SRC = 128
BLK = 512
BF = jnp.bfloat16
F32 = jnp.float32
MESH = pl.DeviceIdType.MESH
VLIM = 56 * 1024 * 1024


def split_bf16(a):
    hi = a.astype(ml_dtypes.bfloat16)
    lo = (a - hi.astype(np.float64)).astype(ml_dtypes.bfloat16)
    return hi, lo


def dft_tables():
    a = np.arange(BLK)[:, None]
    k = np.arange(NFREQ)[None, :] + K_LO
    ang = 2 * np.pi * ((a * k) % (2 * WIN)) / (2 * WIN)
    return split_bf16(np.concatenate([np.cos(ang), -np.sin(ang)], axis=1))


def twiddles():
    b = np.arange(WIN // BLK)[:, None]
    kk = np.arange(256)[None, :]
    ang = 2 * np.pi * ((b * kk * BLK) % (2 * WIN)) / (2 * WIN)
    return np.stack([np.cos(ang), np.sin(ang)], axis=1).astype(np.float32)


def lag_table():
    k = np.arange(NFREQ)[:, None] + K_LO
    i = np.arange(LAGS)[None, :] - LAGS // 2 + 2 * WIN
    ang = 2 * np.pi * ((k * i) % (2 * WIN)) / (2 * WIN)
    t = np.stack([np.cos(ang), -np.sin(ang)]) / math.sqrt(NFREQ * NW)
    t = t.reshape(2, 2, 256, LAGS).transpose(1, 0, 2, 3)
    return t.reshape(2 * NFREQ, LAGS).astype(ml_dtypes.bfloat16)


def band_ones():
    g = np.arange(256) // BANDW
    return (g[:, None] == g[None, :]).astype(ml_dtypes.bfloat16)


def toeplitz(taps):
    d = lax.broadcasted_iota(jnp.int32, (640, 128), 0) - 4 * lax.broadcasted_iota(jnp.int32, (640, 128), 1) - 97
    t = jnp.zeros((640, 128), BF)
    for j in range(TAPS):
        t = jnp.where(d == j, taps[j], t)
    z = jnp.zeros((512, 128), BF)
    return jnp.concatenate([jnp.concatenate([t, z], 0), jnp.concatenate([z, t], 0)], 1)


def dotf(a, b):
    return jnp.dot(a, b, preferred_element_type=F32)


def tdot(a, b):
    return lax.dot_general(a, b, (((0,), (0,)), ((), ())), preferred_element_type=F32)


def hilo(v):
    hi = v.astype(BF)
    return hi, (v - hi.astype(F32)).astype(BF)


def spectra_kernel(x_ref, t_ref, thi_ref, tlo_ref, tw_ref, ones_ref, sel_ref, wst_ref, p_ref, lhs, dhi, dlo):
    rows = x_ref.shape[1]
    lhs[0:rows, 0:128] = jnp.zeros((rows, 128), BF)
    lhs[0:rows, 128:1152] = x_ref[0, :, 0:1024]
    for b in range(1, 16):
        lhs[b * rows:(b + 1) * rows, :] = x_ref[0, :, 1024 * b - 128:1024 * b + 1024]
    d = dotf(lhs[...], t_ref[...])
    for b in range(16):
        hi, lo = hilo(d[b * rows:(b + 1) * rows])
        r0, c0 = (b // 2) * rows, (b % 2) * 256
        dhi[r0:r0 + rows, c0:c0 + 256] = hi
        dlo[r0:r0 + rows, c0:c0 + 256] = lo

    def dot3(c0):
        cols = slice(c0, c0 + 256)
        return dotf(dhi[...], thi_ref[:, cols]) + dotf(dlo[...], thi_ref[:, cols]) + dotf(dhi[...], tlo_ref[:, cols])

    for h in range(2):
        yre = dot3(h * 256)
        yim = dot3(512 + h * 256)
        xre = yre[0:rows]
        xim = yim[0:rows]
        for b in range(1, WIN // BLK):
            c = tw_ref[b, 0:1, :]
            s = tw_ref[b, 1:2, :]
            br = yre[b * rows:(b + 1) * rows]
            bi = yim[b * rows:(b + 1) * rows]
            xre = xre + (br * c + bi * s)
            xim = xim + (bi * c - br * s)
        phi, plo = hilo(xre * xre + xim * xim)
        power = dotf(phi, ones_ref[...]) + dotf(plo, ones_ref[...])
        scale = lax.rsqrt(power * (1.0 / BANDW) + 1e-6)
        wre = (xre * scale).astype(BF)
        wim = (xim * scale).astype(BF)
        for z in range(4):
            wst_ref[h, z, 0, :, 0:256] = wre[16 * z:16 * z + 16]
            wst_ref[h, z, 0, :, 256:512] = wim[16 * z:16 * z + 16]
        for p, part in enumerate((wre, wim)):
            picked = tdot(part, sel_ref[...]).astype(BF)
            for j in range(16):
                p_ref[j, h, 0, p] = picked[16 * j:16 * j + 16]


def spectra(x, toep, sel):
    thi, tlo = dft_tables()
    full = lambda *s: pl.BlockSpec(s, lambda w: (0,) * len(s))
    return pl.pallas_call(
        spectra_kernel,
        grid=(3,),
        in_specs=[
            pl.BlockSpec((1, 64, 4 * WIN), lambda w: (w, 0, 0)),
            full(1152, 256), full(BLK, 1024), full(BLK, 1024), full(8, 2, 256), full(256, 256), full(64, SRC),
        ],
        out_specs=[
            pl.BlockSpec((2, 4, 1, 16, 512), lambda w: (0, 0, w, 0, 0)),
            pl.BlockSpec((16, 2, 1, 2, 16, SRC), lambda w: (0, 0, w, 0, 0, 0)),
        ],
        out_shape=[
            jax.ShapeDtypeStruct((2, 4, 3, 16, 512), BF),
            jax.ShapeDtypeStruct((16, 2, 3, 2, 16, SRC), BF),
        ],
        scratch_shapes=[
            pltpu.VMEM((1024, 1152), BF),
            pltpu.VMEM((512, BLK), BF),
            pltpu.VMEM((512, BLK), BF),
        ],
        compiler_params=pltpu.CompilerParams(vmem_limit_bytes=VLIM),
        name="spectra",
    )(x, toep, jnp.asarray(thi), jnp.asarray(tlo), jnp.asarray(twiddles()), jnp.asarray(band_ones()), sel)


def exchange_kernel(p_ref, wst_ref, s_ref, l_ref, rs, red, zin, rs_send, rs_recv, z_sem, t_send, t_recv,
                    l_send, l_recv, g_send, g_recv, loc):
    m = lax.axis_index("tm")
    ch = lax.axis_index("chan")
    core = m % 2
    zh, xy = ch // 16, ch % 16
    x, y = xy // 4, xy % 4
    barrier = pltpu.get_barrier_semaphore()

    def xy_peer(dx, dy):
        return ((x + dx) % 4) * 4 + (y + dy) % 4

    offs = [(dx, dy) for dx in range(4) for dy in range(4)][1:]
    for dx, dy in offs:
        pl.semaphore_signal(barrier, inc=1, device_id=(m, zh * 16 + xy_peer(dx, dy)), device_id_type=MESH)
    for o in range(1, 8):
        pl.semaphore_signal(barrier, inc=1, device_id=((m + o) % 8, ch), device_id_type=MESH)
    other = (m, (1 - zh) * 16 + xy)
    pl.semaphore_signal(barrier, inc=1, device_id=other, device_id_type=MESH)
    pl.semaphore_wait(barrier, 23)

    def remote(src, dst, ssem, rsem, dev):
        c = pltpu.make_async_remote_copy(src_ref=src, dst_ref=dst, send_sem=ssem, recv_sem=rsem,
                                         device_id=dev, device_id_type=MESH)
        c.start()
        return c

    rs_c = []
    for n, (dx, dy) in enumerate(offs):
        j = xy_peer(dx, dy)
        rs_c.append(remote(p_ref.at[j], rs.at[n], rs_send.at[n], rs_recv.at[n], (m, zh * 16 + j)))
    l_c = []
    for o in range(1, 8):
        mm = (m + o) % 8
        l_c.append(remote(wst_ref.at[mm % 2, mm // 2], l_ref.at[m], l_send.at[o], l_recv.at[o], (mm, ch)))
    own = pltpu.make_async_copy(wst_ref.at[core, m // 2], l_ref.at[m], loc)
    own.start()
    total = p_ref[xy]
    for n in range(15):
        rs_c[n].wait_recv()
        total = total + rs[n]
    red[0] = total
    zc = remote(red.at[0], zin, z_sem.at[0], z_sem.at[1], other)
    zc.wait_recv()
    red[1] = red[0] + zin[...]
    t_c = []
    for o in range(1, 8):
        mm = (m + o) % 8
        t_c.append(remote(red.at[1, mm % 2], s_ref.at[xy, m], t_send.at[o], t_recv.at[o], (mm, ch)))
    s_ref[xy, m] = red[1, core]
    for o in range(1, 8):
        t_c[o - 1].wait_recv()
    own.wait()

    def peer(f, d):
        return zh * 16 + (xy_peer(d, 0) if f == 0 else xy_peer(0, d))

    first = {}
    for f in range(2):
        for d in (1, 3, 2):
            part = s_ref.at[xy, pl.ds(4 * f, 4)]
            first[f, d] = remote(part, part, g_send.at[f, 0, d], g_recv.at[f, 0, d], (m, peer(f, d)))
    second = {}
    for e in (0, 1, 3, 2):
        for f in range(2):
            if e:
                first[f, e].wait_recv()
            src = xy_peer(4 - e, 0) if f == 0 else xy_peer(0, 4 - e)
            for d in (1, 3, 2):
                part = s_ref.at[src, pl.ds(4 * f, 4)]
                second[f, e, d] = remote(part, part, g_send.at[f, 1 + e, d], g_recv.at[f, 1 + e, d],
                                         (m, peer(1 - f, d)))
    for c in second.values():
        c.wait_recv()
    for c in l_c:
        c.wait_recv()
    for c in rs_c + l_c + t_c + [zc] + list(first.values()) + list(second.values()):
        c.wait_send()


def exchange(picks, wst):
    vm = pl.BlockSpec(memory_space=pltpu.VMEM)
    dma = pltpu.SemaphoreType.DMA
    return pl.pallas_call(
        exchange_kernel,
        in_specs=[vm, vm],
        out_specs=[vm, vm],
        out_shape=[
            jax.ShapeDtypeStruct((16, 8, 3, 2, 16, SRC), BF),
            jax.ShapeDtypeStruct((8, 3, 16, 512), BF),
        ],
        scratch_shapes=[
            pltpu.VMEM((15, 2, 3, 2, 16, SRC), BF),
            pltpu.VMEM((2, 2, 3, 2, 16, SRC), BF),
            pltpu.VMEM((2, 3, 2, 16, SRC), BF),
            dma((15,)), dma((15,)), dma((2,)), dma((8,)), dma((8,)), dma((8,)), dma((8,)),
            dma((2, 5, 4)), dma((2, 5, 4)), dma,
        ],
        compiler_params=pltpu.CompilerParams(collective_id=0, has_side_effects=True, vmem_limit_bytes=VLIM),
        name="exchange",
    )(picks, wst)


def cross_kernel(s_ref, l_ref, xf_ref, l32, lt32, lt, a32, x32, xs, send_sem, recv_sem):
    m = lax.axis_index("tm")
    ch = lax.axis_index("chan")
    core = m % 2
    other = (m + 1 - 2 * core, ch)
    barrier = pltpu.get_barrier_semaphore()
    pl.semaphore_signal(barrier, inc=1, device_id=other, device_id_type=MESH)
    l32[...] = l_ref[...].reshape(24, 16, 512).astype(F32)
    for c in range(16):
        mat = l32[:, c, :]
        re, im = mat[:, 0:256], mat[:, 256:512]
        lt32[:, 2 * c, 0:48] = jnp.concatenate([re, im], 0).T
        lt32[:, 2 * c + 1, 0:48] = jnp.concatenate([-im, re], 0).T
    lt[...] = lt32[:, :, 0:48].astype(BF)

    def step(j, carry):
        for w in range(24):
            for p in range(2):
                a32[:, p * 24 + w, :] = s_ref[j, w // 3, w % 3, p].astype(F32)
        for kk in range(16):
            o = dotf(lt[j * 16 + kk], a32[kk].astype(BF))
            x32[:, j * 16 + kk, :] = o
        return carry

    lax.fori_loop(0, 16, step, 0)
    xs[...] = x32[...].astype(BF).reshape(2, 16, 256, SRC)
    pl.semaphore_wait(barrier, 1)
    c = pltpu.make_async_remote_copy(src_ref=xs.at[1 - core], dst_ref=xf_ref.at[core], send_sem=send_sem,
                                     recv_sem=recv_sem, device_id=other, device_id_type=MESH)
    c.start()
    xf_ref[core] = xs[core]
    c.wait()


def cross(s, l):
    vm = pl.BlockSpec(memory_space=pltpu.VMEM)
    dma = pltpu.SemaphoreType.DMA
    return pl.pallas_call(
        cross_kernel,
        in_specs=[vm, vm],
        out_specs=vm,
        out_shape=jax.ShapeDtypeStruct((2, 16, 256, SRC), BF),
        scratch_shapes=[
            pltpu.VMEM((24, 16, 512), F32),
            pltpu.VMEM((256, 32, 128), F32),
            pltpu.VMEM((256, 32, 48), BF),
            pltpu.VMEM((16, 48, SRC), F32),
            pltpu.VMEM((32, 256, SRC), F32),
            pltpu.VMEM((2, 16, 256, SRC), BF),
            dma, dma,
        ],
        compiler_params=pltpu.CompilerParams(collective_id=1, has_side_effects=True, vmem_limit_bytes=VLIM),
        name="cross",
    )(s, l)


def lags_kernel(xf_ref, lt_ref, out_ref):
    for c in range(8):
        a = xf_ref[:, 2 * c:2 * c + 2].reshape(1024, SRC)
        out_ref[:, c, :] = tdot(a, lt_ref[...])


def lags(xf):
    vm = pl.BlockSpec(memory_space=pltpu.VMEM)
    return pl.pallas_call(
        lags_kernel,
        in_specs=[vm, vm],
        out_specs=vm,
        out_shape=jax.ShapeDtypeStruct((SRC, 8, LAGS), F32),
        compiler_params=pltpu.CompilerParams(vmem_limit_bytes=VLIM),
        name="lags",
    )(xf, jnp.asarray(lag_table()))


def on_device(strain_rate, fir_taps, source_channels):
    x = jnp.transpose(strain_rate, (1, 0, 2))
    first = lax.axis_index("chan") * 64
    ids = first + lax.broadcasted_iota(jnp.int32, (64, SRC), 0)
    sel = (ids == source_channels[None, :]).astype(BF)
    wst, picks = spectra(x, toeplitz(fir_taps), sel)
    s, l = exchange(picks, wst)
    xf = cross(s, l)
    return lags(xf)


def solution(mesh):
    placed = (P("chan", "tm", None), P(), P())
    return jax.shard_map(
        on_device,
        mesh=mesh,
        in_specs=placed,
        out_specs=P(None, ("chan", "tm"), None),
        check_vma=False,
    )
```

```python
import functools
import math

import jax
import jax.numpy as jnp
import ml_dtypes
import numpy as np
from jax import lax
from jax.experimental import pallas as pl
from jax.experimental.pallas import tpu as pltpu
from jax.sharding import PartitionSpec as P

WIN = 4096
NFREQ = 512
BANDW = 64
K_LO = 32
LAGS = 1024
TAPS = 32
NW = 24
SRC = 128
BLK = 512
BF = jnp.bfloat16
F32 = jnp.float32
MESH = pl.DeviceIdType.MESH
VLIM = 56 * 1024 * 1024


def split_bf16(a):
    hi = a.astype(ml_dtypes.bfloat16)
    lo = (a - hi.astype(np.float64)).astype(ml_dtypes.bfloat16)
    return hi, lo


def dft_tables():
    u = np.arange(256)[:, None] - 255.5
    ang = 2 * np.pi * u * (np.arange(NFREQ)[None, :] + K_LO) / (2 * WIN)
    out = []
    for t in (np.cos(ang), np.sin(ang)):
        hi, lo = split_bf16(t)
        out.append(np.concatenate([hi, hi, lo], axis=0))
    return np.stack(out)


def twiddles():
    t = np.arange(WIN // BLK)[:, None] * BLK + 255.5
    ang = 2 * np.pi * t * (np.arange(NFREQ)[None, :] + K_LO) / (2 * WIN)
    return np.stack([np.cos(ang), np.sin(ang)], axis=1).astype(np.float32)


def tap_spread():
    j, a, l = np.ogrid[0:TAPS, 0:8, 0:128]
    fwd = (l < 10) & (a - 4 * l + 31 == j)
    rev = (l < 10) & (a - 4 * (9 - l) + 31 == j)
    return np.stack([fwd, rev], axis=1).reshape(TAPS, 2048).astype(ml_dtypes.bfloat16)


def lag_table():
    k = np.arange(NFREQ)[:, None] + K_LO
    i = np.arange(LAGS)[None, :] - LAGS // 2 + 2 * WIN
    ang = 2 * np.pi * ((k * i) % (2 * WIN)) / (2 * WIN)
    t = np.stack([np.cos(ang), -np.sin(ang)]) / math.sqrt(NFREQ * NW)
    t = t.reshape(2, 2, 256, LAGS).transpose(1, 0, 2, 3)
    return t.reshape(2 * NFREQ, LAGS).astype(ml_dtypes.bfloat16)


def band_ones():
    g = np.arange(256) // BANDW
    return (g[:, None] == g[None, :]).astype(ml_dtypes.bfloat16)


def dotf(a, b):
    return jnp.dot(a, b, preferred_element_type=F32)


def tdot(a, b):
    return lax.dot_general(a, b, (((0,), (0,)), ((), ())), preferred_element_type=F32)


def hilo(v):
    hi = v.astype(BF)
    return hi, (v - hi.astype(F32)).astype(BF)


def band_rows(unit, start, lane_tile):
    lane = lax.broadcasted_iota(jnp.int32, (8, 128), 1) + 128 * lane_tile
    lo, hi = 128 * lane_tile, 128 * lane_tile + 127
    if start > hi or start + 9 < lo:
        return jnp.zeros((8, 128), F32)
    moved = pltpu.roll(unit, start % 128, 1) if start % 128 else unit
    return jnp.where((lane >= start) & (lane < start + 10), moved, 0.0)


def build_bands(taps, spread, bands):
    row = dotf(taps, spread)
    for v in range(2):
        unit = jnp.concatenate([row[0:1, (8 * v + a) * 128:(8 * v + a + 1) * 128] for a in range(8)], axis=0)
        for r in range(0, 144, 2):
            starts = [(2 * q - 32) if v == 0 else (278 - 2 * q) for q in (r, r + 1)]
            for t in range(2):
                rows = jnp.concatenate([band_rows(unit, s, t) for s in starts], axis=0)
                bands[v, 8 * r:8 * r + 16, 128 * t:128 * t + 128] = rows.astype(BF)


def spectra_kernel(x_ref, taps_ref, spread_ref, tab_ref, tw_ref, ones_ref, sel_ref, wst_ref, p_ref,
                   bands, lhs, dcat):
    rows = 64

    @pl.when(pl.program_id(0) == 0)
    def _():
        build_bands(taps_ref[...], spread_ref[...], bands)

    for b in range(16):
        r0 = (b // 2) * rows
        if b == 0:
            lhs[0, 0:rows, 0:128] = jnp.zeros((rows, 128), BF)
            lhs[0, 0:rows, 128:1152] = x_ref[0, :, 0:1024]
        else:
            lhs[b % 2, r0:r0 + rows, :] = x_ref[0, :, 1024 * b - 128:1024 * b + 1024]
    even = dotf(lhs[0], bands[0])
    odd = dotf(lhs[1], bands[1])
    for i, v in enumerate((even + odd, even - odd)):
        hi, lo = hilo(v)
        dcat[i, :, 0:256] = hi
        dcat[i, :, 256:512] = lo
        dcat[i, :, 512:768] = hi

    for h in range(2):
        cols = slice(256 * h, 256 * h + 256)
        yc = dotf(dcat[0], tab_ref[0, :, cols])
        ys = dotf(dcat[1], tab_ref[1, :, cols])
        xre = xim = 0.0
        for b in range(WIN // BLK):
            c = tw_ref[b, 0:1, cols]
            s = tw_ref[b, 1:2, cols]
            bc = yc[b * rows:(b + 1) * rows]
            bs = ys[b * rows:(b + 1) * rows]
            xre = xre + (bc * c - bs * s)
            xim = xim - (bs * c + bc * s)
        phi, plo = hilo(xre * xre + xim * xim)
        power = dotf(phi, ones_ref[...]) + dotf(plo, ones_ref[...])
        scale = lax.rsqrt(power * (1.0 / BANDW) + 1e-6)
        wre = (xre * scale).astype(BF)
        wim = (xim * scale).astype(BF)
        for z in range(4):
            wst_ref[h, z, 0, :, 0:256] = wre[16 * z:16 * z + 16]
            wst_ref[h, z, 0, :, 256:512] = wim[16 * z:16 * z + 16]
        for p, part in enumerate((wre, wim)):
            picked = tdot(part, sel_ref[...]).astype(BF)
            for j in range(16):
                p_ref[h, j // 4, j % 4, 0, p] = picked[16 * j:16 * j + 16]


def spectra(x, taps, sel):
    full = lambda *s: pl.BlockSpec(s, lambda w: (0,) * len(s))
    return pl.pallas_call(
        spectra_kernel,
        grid=(3,),
        in_specs=[
            pl.BlockSpec((1, 64, 4 * WIN), lambda w: (w, 0, 0)),
            full(1, TAPS), full(TAPS, 2048), full(2, 768, NFREQ), full(8, 2, NFREQ), full(256, 256), full(64, SRC),
        ],
        out_specs=[
            pl.BlockSpec((2, 4, 1, 16, 512), lambda w: (0, 0, w, 0, 0)),
            pl.BlockSpec((2, 4, 4, 1, 2, 16, SRC), lambda w: (0, 0, 0, w, 0, 0, 0)),
        ],
        out_shape=[
            jax.ShapeDtypeStruct((2, 4, 3, 16, 512), BF),
            jax.ShapeDtypeStruct((2, 4, 4, 3, 2, 16, SRC), BF),
        ],
        scratch_shapes=[
            pltpu.VMEM((2, 1152, 256), BF),
            pltpu.VMEM((2, 512, 1152), BF),
            pltpu.VMEM((2, 512, 768), BF),
        ],
        compiler_params=pltpu.CompilerParams(vmem_limit_bytes=VLIM),
        name="spectra",
    )(x, taps, jnp.asarray(tap_spread()), jnp.asarray(dft_tables()), jnp.asarray(twiddles()),
      jnp.asarray(band_ones()), sel)


def swap_blocks(vs):
    lane = lax.broadcasted_iota(jnp.int32, vs[0].shape, 1) // 16
    for bit in (1, 2, 4):
        low = lane & bit == 0
        out = list(vs)
        for i in range(8):
            if i & bit == 0:
                a, b = vs[i], vs[i + bit]
                out[i] = jnp.where(low, a, pltpu.roll(b, 16 * bit, 1))
                out[i + bit] = jnp.where(low, pltpu.roll(a, 128 - 16 * bit, 1), b)
        vs = out
    return vs


def build_left(l_buf, u, left):
    odd = (lax.broadcasted_iota(jnp.int32, (16, 128), 1) // 16) % 2 == 1
    for q in range(2):
        for g in range(6):
            vs = []
            for i in range(8):
                w, p = (8 * g + i) // 2, i % 2
                vs.append(l_buf[w // 3, w % 3, :, 256 * p + 128 * q:256 * p + 128 * q + 128].astype(F32))
            for j, v in enumerate(swap_blocks(vs)):
                turned = jnp.where(odd, pltpu.roll(v, 16, 1), -pltpu.roll(v, 112, 1))
                u[0, 8 * q + j, :, 128 * g:128 * g + 128] = v
                u[1, 8 * q + j, :, 128 * g:128 * g + 128] = turned
    diag = lax.broadcasted_iota(jnp.int32, (16, 768), 1) % 16 == lax.broadcasted_iota(jnp.int32, (16, 768), 0)

    def expand(j, carry):
        for c in range(16):
            for p in range(2):
                row = jnp.broadcast_to(u[p, j, c:c + 1, :], (16, 768))
                r0 = (2 * c + p) * 16
                left[j, r0:r0 + 16, :] = jnp.where(diag, row, 0.0).astype(BF)
        return carry

    lax.fori_loop(0, 16, expand, 0)


def exchange_kernel(p_ref, wst_ref, xf_ref, r1, acc, r2, red, zin, s_buf, l_buf, u, left, xs,
                    r_send, r_recv, z_sem, t_send, t_recv, l_send, l_recv, g_send, g_recv, x_sem, loc):
    m = lax.axis_index("tm")
    ch = lax.axis_index("chan")
    core = m % 2
    zh, xy = ch // 16, ch % 16
    x, y = xy // 4, xy % 4
    barrier = pltpu.get_barrier_semaphore()

    def xy_peer(dx, dy):
        return ((x + dx) % 4) * 4 + (y + dy) % 4

    def along(axis, d):
        return (m, zh * 16 + (xy_peer(d, 0) if axis == 0 else xy_peer(0, d)))

    other_z = (m, (1 - zh) * 16 + xy)
    other_core = (m + 1 - 2 * core, ch)
    for axis in range(2):
        for d in (1, 2, 3):
            pl.semaphore_signal(barrier, inc=1, device_id=along(axis, d), device_id_type=MESH)
    for o in range(1, 8):
        pl.semaphore_signal(barrier, inc=1, device_id=((m + o) % 8, ch), device_id_type=MESH)
    pl.semaphore_signal(barrier, inc=1, device_id=other_z, device_id_type=MESH)
    pl.semaphore_wait(barrier, 14)
    copies = []

    def remote(src, dst, ssem, rsem, dev):
        c = pltpu.make_async_remote_copy(src_ref=src, dst_ref=dst, send_sem=ssem, recv_sem=rsem,
                                         device_id=dev, device_id_type=MESH)
        c.start()
        copies.append(c)
        return c

    def chunk(f, d):
        return p_ref.at[0, (x + d) % 4] if f == 0 else p_ref.at[1, :, (y + d) % 4]

    mine = (x, y)
    got = {}
    for d in (2, 1, 3):
        for f in range(2):
            got[f, d] = remote(chunk(f, d), r1.at[f, d - 1], r_send.at[f, 0, d - 1],
                               r_recv.at[f, 0, d - 1], along(f, d))
    l_c = []
    for o in range(1, 8):
        mm = (m + o) % 8
        l_c.append(remote(wst_ref.at[mm % 2, mm // 2], l_buf.at[m], l_send.at[o], l_recv.at[o], (mm, ch)))
    own = pltpu.make_async_copy(wst_ref.at[core, m // 2], l_buf.at[m], loc)
    own.start()
    got2 = {}
    for f in range(2):
        for d in (1, 3, 2):
            got[f, d].wait_recv()
        acc[f] = chunk(f, 0)[...] + r1[f, 0] + r1[f, 1] + r1[f, 2]
        for d in (2, 1, 3):
            got2[f, d] = remote(acc.at[f, (mine[1 - f] + d) % 4], r2.at[f, d - 1], r_send.at[f, 1, d - 1],
                                r_recv.at[f, 1, d - 1], along(1 - f, d))
    for f in range(2):
        for d in (1, 3, 2):
            got2[f, d].wait_recv()
        red[0, f] = acc[f, mine[1 - f]] + r2[f, 0] + r2[f, 1] + r2[f, 2]
    remote(red.at[0], zin, z_sem.at[0], z_sem.at[1], other_z).wait_recv()
    red[1] = red[0] + zin[...]
    t_c = []
    for o in range(1, 8):
        mm = (m + o) % 8
        t_c.append(remote(red.at[1, mm % 2], s_buf.at[xy, m], t_send.at[o], t_recv.at[o], (mm, ch)))
    s_buf[xy, m] = red[1, core]
    own.wait()
    for c in l_c:
        c.wait_recv()
    build_left(l_buf, u, left)
    for c in t_c:
        c.wait_recv()

    arrived = {}

    def mark(f, a, b, n):
        key = (a, b) if f == 0 else (b, a)
        arrived[key] = arrived.get(key, 0) + n
        if arrived[key] == 4:
            j = xy_peer(*key)
            o = dotf(left[j], s_buf[j].reshape(768, SRC))
            xs[:, j] = o.astype(BF).reshape(32, 16, SRC)

    def shard(f, a, b):
        return xy_peer(a, b) if f == 0 else xy_peer(b, a)

    def send(f, src, first, count, slot, d, axis):
        part = s_buf.at[src, pl.ds(4 * f + first, count)]
        return remote(part, part, g_send.at[f, slot], g_recv.at[f, slot], along(axis, d))

    c1, c2 = {}, {}

    def second(f, a, slot):
        c2[f, a, 1] = send(f, shard(f, a, 0), 0, 4, slot, 1, 1 - f)
        c2[f, a, 3] = send(f, shard(f, a, 0), 0, 4, slot + 1, 3, 1 - f)

    def forward(f, a, slot):
        c2[f, a, 1].wait_recv()
        c2[f, a, 4] = send(f, shard(f, a, 3), 0, 2, slot + 2, 1, 1 - f)
        c2[f, a, 3].wait_recv()
        c2[f, a, 5] = send(f, shard(f, a, 1), 2, 2, slot + 3, 3, 1 - f)

    def finish(f, a):
        c2[f, a, 4].wait_recv()
        c2[f, a, 5].wait_recv()

    for f in range(2):
        c1[f, 1] = send(f, xy, 0, 4, 0, 1, f)
        c1[f, 3] = send(f, xy, 0, 4, 1, 3, f)
    for f in range(2):
        second(f, 0, 4)
    mark(0, 0, 0, 4)
    for f in range(2):
        c1[f, 1].wait_recv()
        c1[f, 4] = send(f, shard(f, 3, 0), 0, 2, 2, 1, f)
        c1[f, 3].wait_recv()
        c1[f, 5] = send(f, shard(f, 1, 0), 2, 2, 3, 3, f)
    for f in range(2):
        second(f, 3, 8)
        second(f, 1, 12)
    for f in range(2):
        forward(f, 0, 4)
    for f in range(2):
        c1[f, 4].wait_recv()
        c1[f, 5].wait_recv()
        second(f, 2, 16)
    for f in range(2):
        for a in (1, 3, 2):
            mark(f, a, 0, 2)
        for b in (1, 3):
            mark(f, 0, b, 2)
    for f in range(2):
        forward(f, 3, 8)
    for f in range(2):
        finish(f, 0)
        mark(f, 0, 2, 2)
    for f in range(2):
        forward(f, 1, 12)
    for f in range(2):
        for a in (1, 3):
            for b in (1, 3):
                mark(f, a, b, 2)
    for f in range(2):
        forward(f, 2, 16)
        mark(f, 2, 1, 2)
        mark(f, 2, 3, 2)
    for a in (3, 1, 2):
        for f in range(2):
            finish(f, a)
            mark(f, a, 2, 2)

    xc = remote(xs.at[pl.ds((1 - core) * 16, 16)], xf_ref.at[core], x_sem.at[0], x_sem.at[1], other_core)
    xf_ref[core] = xs[pl.ds(core * 16, 16)]
    xc.wait_recv()
    for c in copies:
        c.wait_send()


def exchange(picks, wst):
    vm = pl.BlockSpec(memory_space=pltpu.VMEM)
    dma = pltpu.SemaphoreType.DMA
    tile = (3, 2, 16, SRC)
    return pl.pallas_call(
        exchange_kernel,
        in_specs=[vm, vm],
        out_specs=vm,
        out_shape=jax.ShapeDtypeStruct((2, 16, 16, 16, SRC), BF),
        scratch_shapes=[
            pltpu.VMEM((2, 3, 4) + tile, BF),
            pltpu.VMEM((2, 4) + tile, BF),
            pltpu.VMEM((2, 3) + tile, BF),
            pltpu.VMEM((2, 2) + tile, BF),
            pltpu.VMEM((2,) + tile, BF),
            pltpu.VMEM((16, 8) + tile, BF),
            pltpu.VMEM((8, 3, 16, 512), BF),
            pltpu.VMEM((2, 16, 16, 768), F32),
            pltpu.VMEM((16, 512, 768), BF),
            pltpu.VMEM((32, 16, 16, SRC), BF),
            dma((2, 2, 3)), dma((2, 2, 3)), dma((2,)), dma((8,)), dma((8,)), dma((8,)), dma((8,)),
            dma((2, 20)), dma((2, 20)), dma((2,)), dma,
        ],
        compiler_params=pltpu.CompilerParams(collective_id=0, has_side_effects=True, vmem_limit_bytes=VLIM),
        name="exchange",
    )(picks, wst)


def lags_kernel(xf_ref, lt_ref, out_ref, lhs):
    @pl.when(pl.program_id(0) == 0)
    def _():
        for c in range(8):
            lhs[c * SRC:(c + 1) * SRC, :] = xf_ref[:, 2 * c:2 * c + 2].reshape(1024, SRC).T

    o = dotf(lhs[...], lt_ref[...])
    for c in range(8):
        out_ref[:, c, :] = o[c * SRC:(c + 1) * SRC]


def lags(xf):
    return pl.pallas_call(
        lags_kernel,
        grid=(4,),
        in_specs=[
            pl.BlockSpec((2, 16, 256, SRC), lambda n: (0, 0, 0, 0)),
            pl.BlockSpec((1024, 256), lambda n: (0, n)),
        ],
        out_specs=pl.BlockSpec((SRC, 8, 256), lambda n: (0, 0, n)),
        out_shape=jax.ShapeDtypeStruct((SRC, 8, LAGS), F32),
        scratch_shapes=[pltpu.VMEM((1024, 1024), BF)],
        compiler_params=pltpu.CompilerParams(vmem_limit_bytes=VLIM),
        name="lags",
    )(xf, jnp.asarray(lag_table()))


def on_device(strain_rate, fir_taps, source_channels):
    x = jnp.transpose(strain_rate, (1, 0, 2))
    first = lax.axis_index("chan") * 64
    ids = first + lax.broadcasted_iota(jnp.int32, (64, SRC), 0)
    sel = (ids == source_channels[None, :]).astype(BF)
    wst, picks = spectra(x, fir_taps.reshape(1, TAPS), sel)
    xf = exchange(picks, wst)
    return lags(xf.reshape(2, 16, 256, SRC))


def solution(mesh):
    placed = (P("chan", "tm", None), P(), P())
    return jax.shard_map(
        on_device,
        mesh=mesh,
        in_specs=placed,
        out_specs=P(None, ("chan", "tm"), None),
        check_vma=False,
    )
```

```python
import functools
import math

import jax
import jax.numpy as jnp
import ml_dtypes
import numpy as np
from jax import lax
from jax.experimental import pallas as pl
from jax.experimental.pallas import tpu as pltpu
from jax.sharding import PartitionSpec as P

WIN = 4096
NFREQ = 512
BANDW = 64
K_LO = 32
LAGS = 1024
TAPS = 32
NW = 24
SRC = 128
BLK = 512
BF = jnp.bfloat16
F32 = jnp.float32
MESH = pl.DeviceIdType.MESH
VLIM = 56 * 1024 * 1024


def split_bf16(a):
    hi = a.astype(ml_dtypes.bfloat16)
    lo = (a - hi.astype(np.float64)).astype(ml_dtypes.bfloat16)
    return hi, lo


def dft_tables():
    u = np.arange(256)[:, None] - 255.5
    ang = 2 * np.pi * u * (np.arange(NFREQ)[None, :] + K_LO) / (2 * WIN)
    out = []
    for t in (np.cos(ang), np.sin(ang)):
        hi, lo = split_bf16(t)
        out.append(np.concatenate([hi, hi, lo], axis=0))
    return np.stack(out)


def twiddles():
    t = np.arange(WIN // BLK)[:, None] * BLK + 255.5
    ang = 2 * np.pi * t * (np.arange(NFREQ)[None, :] + K_LO) / (2 * WIN)
    return np.stack([np.cos(ang), np.sin(ang)], axis=1).astype(np.float32)


def tap_spread():
    j, a, l = np.ogrid[0:TAPS, 0:8, 0:128]
    fwd = (l < 10) & (a - 4 * l + 31 == j)
    rev = (l < 10) & (a - 4 * (9 - l) + 31 == j)
    return np.stack([fwd, rev], axis=1).reshape(TAPS, 2048).astype(ml_dtypes.bfloat16)


def lag_table():
    k = np.arange(NFREQ)[:, None] + K_LO
    i = np.arange(LAGS)[None, :] - LAGS // 2 + 2 * WIN
    ang = 2 * np.pi * ((k * i) % (2 * WIN)) / (2 * WIN)
    t = np.stack([np.cos(ang), -np.sin(ang)]) / math.sqrt(NFREQ * NW)
    t = t.reshape(2, 2, 256, LAGS).transpose(1, 0, 2, 3)
    return t.reshape(2 * NFREQ, LAGS).astype(ml_dtypes.bfloat16)


def band_ones():
    g = np.arange(256) // BANDW
    return (g[:, None] == g[None, :]).astype(ml_dtypes.bfloat16)


def dotf(a, b):
    return jnp.dot(a, b, preferred_element_type=F32)


def tdot(a, b):
    return lax.dot_general(a, b, (((0,), (0,)), ((), ())), preferred_element_type=F32)


def hilo(v):
    hi = v.astype(BF)
    return hi, (v - hi.astype(F32)).astype(BF)


def band_rows(unit, start, lane_tile):
    lane = lax.broadcasted_iota(jnp.int32, (8, 128), 1) + 128 * lane_tile
    lo, hi = 128 * lane_tile, 128 * lane_tile + 127
    if start > hi or start + 9 < lo:
        return jnp.zeros((8, 128), F32)
    moved = pltpu.roll(unit, start % 128, 1) if start % 128 else unit
    return jnp.where((lane >= start) & (lane < start + 10), moved, 0.0)


def build_bands(taps, spread, bands):
    row = dotf(taps, spread)
    for v in range(2):
        unit = jnp.concatenate([row[0:1, (8 * v + a) * 128:(8 * v + a + 1) * 128] for a in range(8)], axis=0)
        for r in range(0, 144, 2):
            starts = [(2 * q - 32) if v == 0 else (278 - 2 * q) for q in (r, r + 1)]
            for t in range(2):
                rows = jnp.concatenate([band_rows(unit, s, t) for s in starts], axis=0)
                bands[v, 8 * r:8 * r + 16, 128 * t:128 * t + 128] = rows.astype(BF)


def swap_blocks(vs):
    lane = lax.broadcasted_iota(jnp.int32, vs[0].shape, 1) // 16
    for bit in (1, 2, 4):
        low = lane & bit == 0
        out = list(vs)
        for i in range(8):
            if i & bit == 0:
                a, b = vs[i], vs[i + bit]
                out[i] = jnp.where(low, a, pltpu.roll(b, 16 * bit, 1))
                out[i + bit] = jnp.where(low, pltpu.roll(a, 128 - 16 * bit, 1), b)
        vs = out
    return vs


def build_left(w, l_buf, u, left):
    odd = (lax.broadcasted_iota(jnp.int32, (16, 128), 1) // 16) % 2 == 1
    for q in range(2):
        for g in range(2):
            vs = []
            for i in range(8):
                m, p = 4 * g + i // 2, i % 2
                vs.append(l_buf[w, m, :, 256 * p + 128 * q:256 * p + 128 * q + 128].astype(F32))
            for j, v in enumerate(swap_blocks(vs)):
                turned = jnp.where(odd, pltpu.roll(v, 16, 1), -pltpu.roll(v, 112, 1))
                u[0, 8 * q + j, :, 128 * g:128 * g + 128] = v
                u[1, 8 * q + j, :, 128 * g:128 * g + 128] = turned
    diag = lax.broadcasted_iota(jnp.int32, (16, 256), 1) % 16 == lax.broadcasted_iota(jnp.int32, (16, 256), 0)

    def expand(j, carry):
        for c in range(16):
            for p in range(2):
                row = jnp.broadcast_to(u[p, j, c:c + 1, :], (16, 256))
                r0 = (2 * c + p) * 16
                left[j, r0:r0 + 16, 256 * w:256 * w + 256] = jnp.where(diag, row, 0.0).astype(BF)
        return carry

    lax.fori_loop(0, 16, expand, 0)


def filter_window(x, bands, lhs, dcat):
    rows = 64
    for b in range(16):
        r0 = (b // 2) * rows
        if b == 0:
            lhs[0, 0:rows, 0:128] = jnp.zeros((rows, 128), BF)
            lhs[0, 0:rows, 128:1152] = x[:, 0:1024]
        else:
            lhs[b % 2, r0:r0 + rows, :] = x[:, 1024 * b - 128:1024 * b + 1024]
    even = dotf(lhs[0], bands[0])
    odd = dotf(lhs[1], bands[1])
    for i, v in enumerate((even + odd, even - odd)):
        hi, lo = hilo(v)
        dcat[i, :, 0:256] = hi
        dcat[i, :, 256:512] = lo
        dcat[i, :, 512:768] = hi


def spectrum_half(h, dcat, tab, tw, ones, sel, wst, picks):
    rows = 64
    cols = slice(256 * h, 256 * h + 256)
    yc = dotf(dcat[0], tab[0, :, cols])
    ys = dotf(dcat[1], tab[1, :, cols])
    xre = xim = 0.0
    for b in range(WIN // BLK):
        c = tw[b, 0:1, cols]
        s = tw[b, 1:2, cols]
        bc = yc[b * rows:(b + 1) * rows]
        bs = ys[b * rows:(b + 1) * rows]
        xre = xre + (bc * c - bs * s)
        xim = xim - (bs * c + bc * s)
    phi, plo = hilo(xre * xre + xim * xim)
    power = dotf(phi, ones[...]) + dotf(plo, ones[...])
    scale = lax.rsqrt(power * (1.0 / BANDW) + 1e-6)
    wre = (xre * scale).astype(BF)
    wim = (xim * scale).astype(BF)
    for z in range(4):
        wst[h, z, :, 0:256] = wre[16 * z:16 * z + 16]
        wst[h, z, :, 256:512] = wim[16 * z:16 * z + 16]
    for p, part in enumerate((wre, wim)):
        picked = tdot(part, sel).astype(BF)
        for j in range(16):
            picks[h, j // 4, j % 4, p] = picked[16 * j:16 * j + 16]


def cross_kernel(x_hbm, tab_hbm, taps_ref, spread_ref, tw, ones, src_ref, xf_ref,
                 x_buf, tab, bands, lhs, dcat, picks, wst, r1, acc, r2, red, zin, s_buf, l_buf, u, left, part, xs,
                 in_sem, p_send, p_recv, z_send, z_recv, t_send, t_recv, l_send, l_recv, l_own, g_send, g_recv,
                 x_sem):
    m = lax.axis_index("tm")
    ch = lax.axis_index("chan")
    core = m % 2
    zl = m // 2
    zh, xy = ch // 16, ch % 16
    x, y = xy // 4, xy % 4
    z = zh * 4 + zl
    barrier = pltpu.get_barrier_semaphore()
    loads = [pltpu.make_async_copy(tab_hbm, tab, in_sem.at[3])]
    loads += [pltpu.make_async_copy(x_hbm.at[w], x_buf.at[w], in_sem.at[w]) for w in range(3)]
    for n in (1, 0, 2, 3):
        loads[n].start()

    def xy_peer(dx, dy):
        return ((x + dx) % 4) * 4 + (y + dy) % 4

    def along(axis, d):
        return (m, zh * 16 + (xy_peer(d, 0) if axis == 0 else xy_peer(0, d)))

    def on_ring(d, to_core):
        zz = (z + d) % 8
        return ((zz % 4) * 2 + to_core, (zz // 4) * 16 + xy)

    for axis in range(2):
        for d in (1, 2, 3):
            pl.semaphore_signal(barrier, inc=1, device_id=along(axis, d), device_id_type=MESH)
    for d in range(8):
        for flip in range(2):
            if d or flip:
                pl.semaphore_signal(barrier, inc=1, device_id=on_ring(d, (core + flip) % 2), device_id_type=MESH)

    def remote(src, dst, ssem, rsem, dev):
        pltpu.make_async_remote_copy(src_ref=src, dst_ref=dst, send_sem=ssem, recv_sem=rsem,
                                     device_id=dev, device_id_type=MESH).start()

    def take(ref, sem):
        pltpu.make_async_copy(ref, ref, sem).wait()

    ids = ch * 64 + lax.broadcasted_iota(jnp.int32, (64, SRC), 0)
    sel = (ids == src_ref[...]).astype(F32).astype(BF)
    build_bands(taps_ref[...], spread_ref[...], bands)
    mine = (x, y)
    arrived = {}

    def mark(w, a, b):
        for f in range(2):
            key = (a, b) if f == 0 else (b, a)
            arrived[w, key] = arrived.get((w, key), 0) + 1
            if arrived[w, key] < 2 or w == 0:
                continue
            j = xy_peer(*key)
            if w == 1:
                part[j] = dotf(left[j, :, 0:512], s_buf[j, 0:2].reshape(512, SRC))
                continue
            o = part[j] + dotf(left[j, :, 512:768], s_buf[j, 2].reshape(256, SRC))
            xs[:, j] = o.astype(BF).reshape(32, 16, SRC)
            remote(xs.at[pl.ds((1 - core) * 16, 16), j], xf_ref.at[core, :, j], x_sem.at[0], x_sem.at[1],
                   (m + 1 - 2 * core, ch))
            pltpu.make_async_copy(xs.at[pl.ds(core * 16, 16), j], xf_ref.at[core, :, j], x_sem.at[2]).start()

    def chain(w):
        def chunk(f, d):
            return picks.at[w, 0, (x + d) % 4] if f == 0 else picks.at[w, 1, :, (y + d) % 4]

        for d in (2, 1, 3):
            for f in range(2):
                remote(chunk(f, d), r1.at[w, f, d - 1], p_send.at[w, 0], p_recv.at[w, 0, f], along(f, d))
        for o in range(1, 8):
            mm = (m + o) % 8
            remote(wst.at[w, mm % 2, mm // 2], l_buf.at[w, m], l_send.at[w], l_recv.at[w], (mm, ch))
        pltpu.make_async_copy(wst.at[w, core, zl], l_buf.at[w, m], l_own.at[w]).start()
        yield
        for f in range(2):
            take(r1.at[w, f], p_recv.at[w, 0, f])
            acc[w, f] = chunk(f, 0)[...] + r1[w, f, 0] + r1[w, f, 1] + r1[w, f, 2]
            for d in (2, 1, 3):
                remote(acc.at[w, f, (mine[1 - f] + d) % 4], r2.at[w, f, d - 1], p_send.at[w, 1],
                       p_recv.at[w, 1, f], along(1 - f, d))
        yield
        for f in range(2):
            take(r2.at[w, f], p_recv.at[w, 1, f])
            red[w, 0, f] = acc[w, f, mine[1 - f]] + r2[w, f, 0] + r2[w, f, 1] + r2[w, f, 2]
        remote(red.at[w, 0], zin.at[w], z_send.at[w], z_recv.at[w], on_ring(4, core))
        yield
        take(zin.at[w], z_recv.at[w])
        red[w, 1] = red[w, 0] + zin[w]
        for d in (2 - 4 * core, 1, -1):
            for flip in range(2):
                to = (core + flip) % 2
                remote(red.at[w, 1, to], s_buf.at[xy, w, m], t_send.at[w], t_recv.at[w], on_ring(d + 8, to))
        remote(red.at[w, 1, 1 - core], s_buf.at[xy, w, m], t_send.at[w], t_recv.at[w], on_ring(0, 1 - core))
        s_buf[xy, w, m] = red[w, 1, core]
        yield
        take(s_buf.at[xy, w, pl.ds(0, 7)], t_recv.at[w])

        def send(f, a, b, slot, d, axis):
            src = xy_peer(a, b) if f == 0 else xy_peer(b, a)
            part = s_buf.at[src, w, pl.ds(4 * f, 4)]
            remote(part, part, g_send.at[w], g_recv.at[w, slot], along(axis, d))

        def second(f, a, slot):
            send(f, a, 0, slot, 1, 1 - f)
            send(f, a, 0, slot, 3, 1 - f)

        def forward(f, a, slot):
            first = 1 if a % 2 == 0 else 3
            send(f, a, 4 - first, slot, first, 1 - f)

        def got(shards, slot):
            take(s_buf.at[pl.ds(0, shards), w], g_recv.at[w, slot])

        for f in range(2):
            send(f, 0, 0, 0, 1, f)
            send(f, 0, 0, 0, 3, f)
        for f in range(2):
            second(f, 0, 2)
        mark(w, 0, 0)
        yield
        got(2, 0)
        for f in range(2):
            first = 1 if f == 0 else 3
            send(f, 4 - first, 0, 1, first, f)
        for f in range(2):
            second(f, 3, 4)
            second(f, 1, 4)
        got(2, 2)
        for f in range(2):
            forward(f, 0, 3)
        for a in (1, 3):
            mark(w, a, 0)
            mark(w, 0, a)
        yield
        got(1, 1)
        for f in range(2):
            second(f, 2, 6)
        got(4, 4)
        for a in (3, 1):
            for f in range(2):
                forward(f, a, 5)
        mark(w, 2, 0)
        for a in (1, 3):
            for b in (1, 3):
                mark(w, a, b)
        yield
        got(2, 6)
        for f in range(2):
            forward(f, 2, 7)
        got(1, 3)
        mark(w, 0, 2)
        got(2, 5)
        for a in (1, 3):
            mark(w, 2, a)
            mark(w, a, 2)
        yield
        got(1, 7)
        mark(w, 2, 2)
        yield

    def filt(w):
        loads[1 + w].wait()
        filter_window(x_buf.at[w], bands, lhs, dcat)

    def half(w, h):
        spectrum_half(h, dcat, tab, tw, ones, sel, wst.at[w], picks.at[w])

    def build(w):
        take(l_buf.at[w, m], l_own.at[w])
        take(l_buf.at[w, pl.ds(0, 7)], l_recv.at[w])
        build_left(w, l_buf, u, left)

    chains = [chain(w) for w in range(3)]

    def go(*ws):
        for w in ws:
            next(chains[w])

    filt(0)
    loads[0].wait()
    half(0, 0)
    half(0, 1)
    pl.semaphore_wait(barrier, 21)
    go(0)
    filt(1)
    half(1, 0)
    half(1, 1)
    go(0, 1)
    filt(2)
    half(2, 0)
    half(2, 1)
    go(0, 2, 1, 2, 1, 0, 2, 0)
    build(0)
    go(1)
    build(1)
    go(0)
    build(2)
    go(1, 2, 0, 2, 1, 2, 1, 0, 2, 1, 2, 0, 1, 2)
    for w in range(3):
        take(r1.at[w], p_send.at[w, 0])
        take(r2.at[w], p_send.at[w, 1])
        take(l_buf.at[w, pl.ds(0, 7)], l_send.at[w])
        take(zin.at[w], z_send.at[w])
        take(s_buf.at[xy, w, pl.ds(0, 7)], t_send.at[w])
        take(s_buf.at[pl.ds(0, 15), w], g_send.at[w])
    for n in range(3):
        take(xs.at[pl.ds(0, 16)], x_sem.at[n])


def cross(x, taps, src):
    vm = pl.BlockSpec(memory_space=pltpu.VMEM)
    hbm = pl.BlockSpec(memory_space=pl.ANY)
    dma = pltpu.SemaphoreType.DMA
    tile = (2, 16, SRC)
    return pl.pallas_call(
        cross_kernel,
        in_specs=[hbm, hbm, vm, vm, vm, vm, vm],
        out_specs=hbm,
        out_shape=jax.ShapeDtypeStruct((2, 16, 16, 16, SRC), BF),
        scratch_shapes=[
            pltpu.VMEM((3, 64, 4 * WIN), BF),
            pltpu.VMEM((2, 768, NFREQ), BF),
            pltpu.VMEM((2, 1152, 256), BF),
            pltpu.VMEM((2, 512, 1152), BF),
            pltpu.VMEM((2, 512, 768), BF),
            pltpu.VMEM((3, 2, 4, 4) + tile, BF),
            pltpu.VMEM((3, 2, 4, 16, 512), BF),
            pltpu.VMEM((3, 2, 3, 4) + tile, BF),
            pltpu.VMEM((3, 2, 4) + tile, BF),
            pltpu.VMEM((3, 2, 3) + tile, BF),
            pltpu.VMEM((3, 2, 2) + tile, BF),
            pltpu.VMEM((3, 2) + tile, BF),
            pltpu.VMEM((16, 3, 8) + tile, BF),
            pltpu.VMEM((3, 8, 16, 512), BF),
            pltpu.VMEM((2, 16, 16, 256), F32),
            pltpu.VMEM((16, 512, 768), BF),
            pltpu.VMEM((16, 512, SRC), F32),
            pltpu.VMEM((32, 16, 16, SRC), BF),
            dma((4,)), dma((3, 2)), dma((3, 2, 2)), dma((3,)), dma((3,)), dma((3,)), dma((3,)), dma((3,)), dma((3,)),
            dma((3,)), dma((3,)), dma((3, 8)), dma((3,)),
        ],
        compiler_params=pltpu.CompilerParams(collective_id=0, has_side_effects=True, vmem_limit_bytes=VLIM),
        name="cross",
    )(x, jnp.asarray(dft_tables()), taps, jnp.asarray(tap_spread()), jnp.asarray(twiddles()),
      jnp.asarray(band_ones()), src)


def lags_kernel(xf_ref, lt_ref, out_ref, lhs):
    @pl.when(pl.program_id(0) == 0)
    def _():
        for c in range(8):
            lhs[c * SRC:(c + 1) * SRC, :] = xf_ref[:, 2 * c:2 * c + 2].reshape(1024, SRC).T

    o = dotf(lhs[...], lt_ref[...])
    for c in range(8):
        out_ref[:, c, :] = o[c * SRC:(c + 1) * SRC]


def lags(xf):
    return pl.pallas_call(
        lags_kernel,
        grid=(4,),
        in_specs=[
            pl.BlockSpec((2, 16, 256, SRC), lambda n: (0, 0, 0, 0)),
            pl.BlockSpec((1024, 256), lambda n: (0, n)),
        ],
        out_specs=pl.BlockSpec((SRC, 8, 256), lambda n: (0, 0, n)),
        out_shape=jax.ShapeDtypeStruct((SRC, 8, LAGS), F32),
        scratch_shapes=[pltpu.VMEM((1024, 1024), BF)],
        compiler_params=pltpu.CompilerParams(vmem_limit_bytes=VLIM),
        name="lags",
    )(xf, jnp.asarray(lag_table()))


def on_device(strain_rate, fir_taps, source_channels):
    x = jnp.transpose(strain_rate, (1, 0, 2))
    xf = cross(x, fir_taps.reshape(1, TAPS), source_channels.reshape(1, SRC))
    return lags(xf.reshape(2, 16, 256, SRC))


def solution(mesh):
    placed = (P("chan", "tm", None), P(), P())
    return jax.shard_map(
        on_device,
        mesh=mesh,
        in_specs=placed,
        out_specs=P(None, ("chan", "tm"), None),
        check_vma=False,
    )
```

```python
import functools
import math

import jax
import jax.numpy as jnp
import ml_dtypes
import numpy as np
from jax import lax
from jax.experimental import pallas as pl
from jax.experimental.pallas import tpu as pltpu
from jax.sharding import PartitionSpec as P

WIN = 4096
NFREQ = 512
BANDW = 64
K_LO = 32
LAGS = 1024
TAPS = 32
NW = 24
SRC = 128
BLK = 512
TABLE_ROWS = 10240
BF = jnp.bfloat16
F32 = jnp.float32
MESH = pl.DeviceIdType.MESH
VLIM = 56 * 1024 * 1024


def split_bf16(a):
    hi = a.astype(ml_dtypes.bfloat16)
    lo = (a - hi.astype(np.float64)).astype(ml_dtypes.bfloat16)
    return hi, lo


def dft_tables():
    u = np.arange(256)[:, None] - 255.5
    ang = 2 * np.pi * u * (np.arange(NFREQ)[None, :] + K_LO) / (2 * WIN)
    out = []
    for t in (np.cos(ang), np.sin(ang)):
        hi, lo = split_bf16(t)
        out.append(np.concatenate([hi, hi, lo], axis=0))
    return np.stack(out)


def twiddles():
    t = np.arange(WIN // BLK)[:, None] * BLK + 255.5
    ang = 2 * np.pi * t * (np.arange(NFREQ)[None, :] + K_LO) / (2 * WIN)
    return np.stack([np.cos(ang), np.sin(ang)], axis=1).astype(np.float32)


def tap_spread():
    j, a, l = np.ogrid[0:TAPS, 0:8, 0:128]
    fwd = (l < 10) & (a - 4 * l + 31 == j)
    rev = (l < 10) & (a - 4 * (9 - l) + 31 == j)
    return np.stack([fwd, rev], axis=1).reshape(TAPS, 4, 512).transpose(1, 0, 2).reshape(4 * TAPS, 512)


def tables():
    tw = twiddles().reshape(16, NFREQ).astype(np.float64)
    hi, rest = split_bf16(tw)
    mid, lo = split_bf16(tw - hi.astype(np.float64))
    rows = np.zeros((TABLE_ROWS, NFREQ), ml_dtypes.bfloat16)
    rows[0:1536] = dft_tables().reshape(1536, NFREQ)
    rows[1536:1792, 0:256] = band_ones()
    rows[1792:1920] = tap_spread()
    rows[1920:1968] = np.concatenate([hi, mid, lo])
    return rows


def lag_table():
    k = np.arange(NFREQ)[:, None] + K_LO
    i = np.arange(LAGS)[None, :] - LAGS // 2 + 2 * WIN
    ang = 2 * np.pi * ((k * i) % (2 * WIN)) / (2 * WIN)
    t = np.stack([np.cos(ang), -np.sin(ang)]) / math.sqrt(NFREQ * NW)
    t = t.reshape(2, 2, 16, 16, LAGS).transpose(1, 2, 0, 3, 4)
    return t.reshape(2 * NFREQ, LAGS).astype(ml_dtypes.bfloat16)


def band_ones():
    g = np.arange(256) // BANDW
    return (g[:, None] == g[None, :]).astype(ml_dtypes.bfloat16)


def dotf(a, b):
    return jnp.dot(a, b, preferred_element_type=F32)


def tdot(a, b):
    return lax.dot_general(a, b, (((0,), (0,)), ((), ())), preferred_element_type=F32)


def hilo(v):
    hi = v.astype(BF)
    return hi, (v - hi.astype(F32)).astype(BF)


def band_rows(unit, start, lane_tile):
    lane = lax.broadcasted_iota(jnp.int32, (8, 128), 1) + 128 * lane_tile
    lo, hi = 128 * lane_tile, 128 * lane_tile + 127
    if start > hi or start + 9 < lo:
        return jnp.zeros((8, 128), F32)
    moved = pltpu.roll(unit, start % 128, 1) if start % 128 else unit
    return jnp.where((lane >= start) & (lane < start + 10), moved, 0.0)


def build_bands(taps, spread, bands):
    row = jnp.concatenate([dotf(taps, spread[TAPS * n:TAPS * n + TAPS]) for n in range(4)], axis=1)
    for v in range(2):
        unit = jnp.concatenate([row[0:1, (8 * v + a) * 128:(8 * v + a + 1) * 128] for a in range(8)], axis=0)
        for r in range(0, 144, 2):
            starts = [(2 * q - 32) if v == 0 else (278 - 2 * q) for q in (r, r + 1)]
            for t in range(2):
                rows = jnp.concatenate([band_rows(unit, s, t) for s in starts], axis=0)
                bands[v, 8 * r:8 * r + 16, 128 * t:128 * t + 128] = rows.astype(BF)


def swap_blocks(vs):
    lane = lax.broadcasted_iota(jnp.int32, vs[0].shape, 1) // 16
    for bit in (1, 2, 4):
        low = lane & bit == 0
        out = list(vs)
        for i in range(8):
            if i & bit == 0:
                a, b = vs[i], vs[i + bit]
                out[i] = jnp.where(low, a, pltpu.roll(b, 16 * bit, 1))
                out[i + bit] = jnp.where(low, pltpu.roll(a, 128 - 16 * bit, 1), b)
        vs = out
    return vs


def build_left(w, l_buf, u, left):
    odd = (lax.broadcasted_iota(jnp.int32, (16, 128), 1) // 16) % 2 == 1
    for q in range(2):
        for g in range(2):
            vs = []
            for i in range(8):
                m, p = 4 * g + i // 2, i % 2
                vs.append(l_buf[w, m, :, 256 * p + 128 * q:256 * p + 128 * q + 128].astype(F32))
            for j, v in enumerate(swap_blocks(vs)):
                turned = jnp.where(odd, pltpu.roll(v, 16, 1), -pltpu.roll(v, 112, 1))
                u[0, 8 * q + j, :, 128 * g:128 * g + 128] = v
                u[1, 8 * q + j, :, 128 * g:128 * g + 128] = turned
    diag = lax.broadcasted_iota(jnp.int32, (16, 256), 1) % 16 == lax.broadcasted_iota(jnp.int32, (16, 256), 0)

    def expand(j, carry):
        for c in range(16):
            for p in range(2):
                row = jnp.broadcast_to(u[p, j, c:c + 1, :], (16, 256))
                r0 = (2 * c + p) * 16
                left[j, r0:r0 + 16, 256 * w:256 * w + 256] = jnp.where(diag, row, 0.0).astype(BF)
        return carry

    lax.fori_loop(0, 16, expand, 0)


def filter_window(x, bands, lhs, dcat):
    rows = 64
    for b in range(16):
        r0 = (b // 2) * rows
        if b == 0:
            lhs[0, 0:rows, 0:128] = jnp.zeros((rows, 128), BF)
            lhs[0, 0:rows, 128:1152] = x[:, 0:1024]
        else:
            lhs[b % 2, r0:r0 + rows, :] = x[:, 1024 * b - 128:1024 * b + 1024]
    even = dotf(lhs[0], bands[0])
    odd = dotf(lhs[1], bands[1])
    for i, v in enumerate((even + odd, even - odd)):
        hi, lo = hilo(v)
        dcat[i, :, 0:256] = hi
        dcat[i, :, 256:512] = lo
        dcat[i, :, 512:768] = hi


def spectrum_half(h, dcat, tab, tw, ones, sel, wst, picks):
    rows = 64
    cols = slice(256 * h, 256 * h + 256)
    yc = dotf(dcat[0], tab[0:768, cols])
    ys = dotf(dcat[1], tab[768:1536, cols])
    xre = xim = 0.0
    for b in range(WIN // BLK):
        c = tw[2 * b:2 * b + 1, cols]
        s = tw[2 * b + 1:2 * b + 2, cols]
        bc = yc[b * rows:(b + 1) * rows]
        bs = ys[b * rows:(b + 1) * rows]
        xre = xre + (bc * c - bs * s)
        xim = xim - (bs * c + bc * s)
    phi, plo = hilo(xre * xre + xim * xim)
    power = dotf(phi, ones) + dotf(plo, ones)
    scale = lax.rsqrt(power * (1.0 / BANDW) + 1e-6)
    wre = (xre * scale).astype(BF)
    wim = (xim * scale).astype(BF)
    for z in range(4):
        wst[h, z, :, 0:256] = wre[16 * z:16 * z + 16]
        wst[h, z, :, 256:512] = wim[16 * z:16 * z + 16]
    for p, part in enumerate((wre, wim)):
        picked = tdot(part, sel).astype(BF)
        for j in range(16):
            picks[h, j // 4, j % 4, p] = picked[16 * j:16 * j + 16]


def cross_kernel(x_hbm, rows_hbm, small, xf_ref, x_buf, tab, aux, tw, bands, lhs, dcat, picks, wst, r1, acc, r2, red, zin, s_buf, l_buf, u, left, part, xs,
                 in_sem, p_send, p_recv, z_send, z_recv, t_send, t_recv, l_send, l_recv, l_own, g_send, g_recv,
                 x_sem):
    m = lax.axis_index("tm")
    ch = lax.axis_index("chan")
    core = m % 2
    zl = m // 2
    zh, xy = ch // 16, ch % 16
    x, y = xy // 4, xy % 4
    z = zh * 4 + zl
    barrier = pltpu.get_barrier_semaphore()
    loads = [pltpu.make_async_copy(rows_hbm.at[pl.ds(0, 1536)], tab, in_sem.at[3])]
    loads += [pltpu.make_async_copy(x_hbm.at[w], x_buf.at[w], in_sem.at[w]) for w in range(3)]
    aux_load = pltpu.make_async_copy(rows_hbm.at[pl.ds(1536, 432)], aux, in_sem.at[4])
    for c in [aux_load, loads[1], loads[0]] + loads[2:]:
        c.start()

    def xy_peer(dx, dy):
        return ((x + dx) % 4) * 4 + (y + dy) % 4

    def along(axis, d):
        return (m, zh * 16 + (xy_peer(d, 0) if axis == 0 else xy_peer(0, d)))

    def on_ring(d, to_core):
        zz = (z + d) % 8
        return ((zz % 4) * 2 + to_core, (zz // 4) * 16 + xy)

    for axis in range(2):
        for d in (1, 2, 3):
            pl.semaphore_signal(barrier, inc=1, device_id=along(axis, d), device_id_type=MESH)
    for d in range(8):
        for flip in range(2):
            if d or flip:
                pl.semaphore_signal(barrier, inc=1, device_id=on_ring(d, (core + flip) % 2), device_id_type=MESH)

    def remote(src, dst, ssem, rsem, dev):
        pltpu.make_async_remote_copy(src_ref=src, dst_ref=dst, send_sem=ssem, recv_sem=rsem,
                                     device_id=dev, device_id_type=MESH).start()

    def take(ref, sem):
        pltpu.make_async_copy(ref, ref, sem).wait()

    aux_load.wait()
    ids = (ch * 64 + lax.broadcasted_iota(jnp.int32, (64, SRC), 0)).astype(F32)
    sel = jnp.maximum(1.0 - jnp.abs(ids - small[1:2, :]), 0.0).astype(BF)
    tw[...] = aux[384:400].astype(F32) + aux[400:416].astype(F32) + aux[416:432].astype(F32)
    ones = aux[0:256, 0:256]
    build_bands(small[0:1, 0:TAPS].astype(BF), aux[256:384], bands)
    mine = (x, y)
    arrived = {}

    def mark(w, *keys):
        ready = []
        for a, b in keys:
            for f in range(2):
                key = (a, b) if f == 0 else (b, a)
                arrived[w, key] = arrived.get((w, key), 0) + 1
                if arrived[w, key] == 2:
                    ready.append(xy_peer(*key))
        if w == 1:
            for j in ready:
                part[j] = dotf(left[j, :, 0:512], s_buf[j, 0:2].reshape(512, SRC))
        if w == 2:
            for j in ready:
                o = part[j] + dotf(left[j, :, 512:768], s_buf[j, 2].reshape(256, SRC))
                xs[:, j] = o.astype(BF).reshape(2, 16, 16, SRC)
            for j in ready:
                remote(xs.at[1 - core, j], xf_ref.at[core, j], x_sem.at[0], x_sem.at[1], (m + 1 - 2 * core, ch))
                pltpu.make_async_copy(xs.at[core, j], xf_ref.at[core, j], x_sem.at[2]).start()

    def chain(w):
        def chunk(f, d):
            return picks.at[w, 0, (x + d) % 4] if f == 0 else picks.at[w, 1, :, (y + d) % 4]

        for d in (2, 1, 3):
            for f in range(2):
                remote(chunk(f, d), r1.at[w, f, d - 1], p_send.at[w, 0], p_recv.at[w, 0, f], along(f, d))
        for o in range(1, 8):
            mm = (m + o) % 8
            remote(wst.at[w, mm % 2, mm // 2], l_buf.at[w, m], l_send.at[w], l_recv.at[w], (mm, ch))
        pltpu.make_async_copy(wst.at[w, core, zl], l_buf.at[w, m], l_own.at[w]).start()
        yield
        for f in range(2):
            take(r1.at[w, f], p_recv.at[w, 0, f])
            acc[w, f] = chunk(f, 0)[...] + r1[w, f, 0] + r1[w, f, 1] + r1[w, f, 2]
            for d in (2, 1, 3):
                remote(acc.at[w, f, (mine[1 - f] + d) % 4], r2.at[w, f, d - 1], p_send.at[w, 1],
                       p_recv.at[w, 1, f], along(1 - f, d))
        yield
        for f in range(2):
            take(r2.at[w, f], p_recv.at[w, 1, f])
            red[w, 0, f] = acc[w, f, mine[1 - f]] + r2[w, f, 0] + r2[w, f, 1] + r2[w, f, 2]
        remote(red.at[w, 0], zin.at[w], z_send.at[w], z_recv.at[w], on_ring(4, core))
        yield
        take(zin.at[w], z_recv.at[w])
        red[w, 1] = red[w, 0] + zin[w]
        for d in (2 - 4 * core, 1, -1):
            for flip in range(2):
                to = (core + flip) % 2
                remote(red.at[w, 1, to], s_buf.at[xy, w, m], t_send.at[w], t_recv.at[w], on_ring(d + 8, to))
        remote(red.at[w, 1, 1 - core], s_buf.at[xy, w, m], t_send.at[w], t_recv.at[w], on_ring(0, 1 - core))
        s_buf[xy, w, m] = red[w, 1, core]
        yield
        take(s_buf.at[xy, w, pl.ds(0, 7)], t_recv.at[w])

        def send(f, a, b, slot, d, axis):
            src = xy_peer(a, b) if f == 0 else xy_peer(b, a)
            part = s_buf.at[src, w, pl.ds(4 * f, 4)]
            remote(part, part, g_send.at[w], g_recv.at[w, slot], along(axis, d))

        def second(f, a, slot):
            send(f, a, 0, slot, 1, 1 - f)
            send(f, a, 0, slot, 3, 1 - f)

        def forward(f, a, slot):
            first = 1 if a % 2 == 0 else 3
            send(f, a, 4 - first, slot, first, 1 - f)

        def got(shards, slot):
            take(s_buf.at[pl.ds(0, shards), w], g_recv.at[w, slot])

        for f in range(2):
            send(f, 0, 0, 0, 1, f)
            send(f, 0, 0, 0, 3, f)
        for f in range(2):
            second(f, 0, 2)
        mark(w, (0, 0))
        yield
        got(2, 0)
        for f in range(2):
            first = 1 if f == 0 else 3
            send(f, 4 - first, 0, 1, first, f)
        for f in range(2):
            second(f, 3, 4)
            second(f, 1, 4)
        got(2, 2)
        for f in range(2):
            forward(f, 0, 3)
        mark(w, (1, 0), (0, 1), (3, 0), (0, 3))
        yield
        got(1, 1)
        for f in range(2):
            second(f, 2, 6)
        got(4, 4)
        for a in (3, 1):
            for f in range(2):
                forward(f, a, 5)
        mark(w, (2, 0), (1, 1), (1, 3), (3, 1), (3, 3))
        yield
        got(2, 6)
        for f in range(2):
            forward(f, 2, 7)
        got(1, 3)
        got(2, 5)
        mark(w, (0, 2), (2, 1), (1, 2), (2, 3), (3, 2))
        yield
        got(1, 7)
        mark(w, (2, 2))
        yield

    def filt(w):
        loads[1 + w].wait()
        filter_window(x_buf.at[w], bands, lhs, dcat)

    def half(w, h):
        spectrum_half(h, dcat, tab, tw, ones, sel, wst.at[w], picks.at[w])

    def build(w):
        take(l_buf.at[w, m], l_own.at[w])
        take(l_buf.at[w, pl.ds(0, 7)], l_recv.at[w])
        build_left(w, l_buf, u, left)

    chains = [chain(w) for w in range(3)]

    def go(*ws):
        for w in ws:
            next(chains[w])

    filt(0)
    loads[0].wait()
    half(0, 0)
    half(0, 1)
    pl.semaphore_wait(barrier, 21)
    go(0)
    filt(1)
    half(1, 0)
    half(1, 1)
    go(0, 1)
    filt(2)
    half(2, 0)
    half(2, 1)
    go(0, 2, 1, 2, 1, 0, 2, 0)
    build(0)
    go(1)
    build(1)
    go(0)
    build(2)
    go(1, 2, 0, 2, 1, 2, 1, 0, 2, 1, 2, 0, 1, 2)
    for w in range(3):
        take(r1.at[w], p_send.at[w, 0])
        take(r2.at[w], p_send.at[w, 1])
        take(l_buf.at[w, pl.ds(0, 7)], l_send.at[w])
        take(zin.at[w], z_send.at[w])
        take(s_buf.at[xy, w, pl.ds(0, 7)], t_send.at[w])
        take(s_buf.at[pl.ds(0, 15), w], g_send.at[w])
    for n in range(3):
        take(xs.at[0], x_sem.at[n])


def cross(x, small):
    hbm = pl.BlockSpec(memory_space=pltpu.HBM)
    dma = pltpu.SemaphoreType.DMA
    tile = (2, 16, SRC)
    return pl.pallas_call(
        cross_kernel,
        in_specs=[hbm, hbm, pl.BlockSpec(memory_space=pltpu.VMEM)],
        out_specs=pl.BlockSpec(memory_space=pl.ANY),
        out_shape=jax.ShapeDtypeStruct((2, 16, 16, 16, SRC), BF),
        scratch_shapes=[
            pltpu.VMEM((3, 64, 4 * WIN), BF),
            pltpu.VMEM((1536, NFREQ), BF),
            pltpu.VMEM((432, NFREQ), BF),
            pltpu.VMEM((16, NFREQ), F32),
            pltpu.VMEM((2, 1152, 256), BF),
            pltpu.VMEM((2, 512, 1152), BF),
            pltpu.VMEM((2, 512, 768), BF),
            pltpu.VMEM((3, 2, 4, 4) + tile, BF),
            pltpu.VMEM((3, 2, 4, 16, 512), BF),
            pltpu.VMEM((3, 2, 3, 4) + tile, BF),
            pltpu.VMEM((3, 2, 4) + tile, BF),
            pltpu.VMEM((3, 2, 3) + tile, BF),
            pltpu.VMEM((3, 2, 2) + tile, BF),
            pltpu.VMEM((3, 2) + tile, BF),
            pltpu.VMEM((16, 3, 8) + tile, BF),
            pltpu.VMEM((3, 8, 16, 512), BF),
            pltpu.VMEM((2, 16, 16, 256), F32),
            pltpu.VMEM((16, 512, 768), BF),
            pltpu.VMEM((16, 512, SRC), F32),
            pltpu.VMEM((2, 16, 16, 16, SRC), BF),
            dma((5,)), dma((3, 2)), dma((3, 2, 2)), dma((3,)), dma((3,)), dma((3,)), dma((3,)), dma((3,)), dma((3,)),
            dma((3,)), dma((3,)), dma((3, 8)), dma((3,)),
        ],
        compiler_params=pltpu.CompilerParams(collective_id=0, has_side_effects=True, vmem_limit_bytes=50 << 20),
        name="cross",
    )(x, jnp.asarray(tables()), small)


def lags_kernel(xf_ref, lt_ref, out_ref, lhs):
    @pl.when(pl.program_id(0) == 0)
    def _():
        for c in range(8):
            lhs[c * SRC:(c + 1) * SRC, :] = xf_ref[:, :, 2 * c:2 * c + 2].reshape(1024, SRC).T

    o = dotf(lhs[...], lt_ref[...])
    for c in range(8):
        out_ref[:, c, :] = o[c * SRC:(c + 1) * SRC]


def lags(xf):
    return pl.pallas_call(
        lags_kernel,
        grid=(4,),
        in_specs=[
            pl.BlockSpec((2, 16, 16, 16, SRC), lambda n: (0, 0, 0, 0, 0)),
            pl.BlockSpec((1024, 256), lambda n: (0, n)),
        ],
        out_specs=pl.BlockSpec((SRC, 8, 256), lambda n: (0, 0, n)),
        out_shape=jax.ShapeDtypeStruct((SRC, 8, LAGS), F32),
        scratch_shapes=[pltpu.VMEM((1024, 1024), BF)],
        compiler_params=pltpu.CompilerParams(vmem_limit_bytes=24 << 20),
        name="lags",
    )(xf, jnp.asarray(lag_table()))


def on_device(strain_rate, fir_taps, source_channels):
    x = jnp.transpose(strain_rate, (1, 0, 2))
    taps = jnp.pad(fir_taps.astype(F32), (0, SRC - TAPS))
    first = lax.broadcasted_iota(jnp.int32, (2, SRC), 0) == 0
    xf = cross(x, jnp.where(first, taps[None, :], source_channels.astype(F32)[None, :]))
    return lags(xf)


def solution(mesh):
    placed = (P("chan", "tm", None), P(), P())
    return jax.shard_map(
        on_device,
        mesh=mesh,
        in_specs=placed,
        out_specs=P(None, ("chan", "tm"), None),
        check_vma=False,
    )
```

```python
import functools
import math

import jax
import jax.numpy as jnp
import ml_dtypes
import numpy as np
from jax import lax
from jax.experimental import pallas as pl
from jax.experimental.pallas import tpu as pltpu
from jax.sharding import PartitionSpec as P

WIN = 4096
NFREQ = 512
BANDW = 64
K_LO = 32
LAGS = 1024
TAPS = 32
NW = 24
SRC = 128
BLK = 512
TABLE_ROWS = 10240
BF = jnp.bfloat16
F32 = jnp.float32
MESH = pl.DeviceIdType.MESH
VLIM = 56 * 1024 * 1024


def split_bf16(a):
    hi = a.astype(ml_dtypes.bfloat16)
    lo = (a - hi.astype(np.float64)).astype(ml_dtypes.bfloat16)
    return hi, lo


def dft_tables():
    u = np.arange(256)[:, None] - 255.5
    ang = 2 * np.pi * u * (np.arange(NFREQ)[None, :] + K_LO) / (2 * WIN)
    out = []
    for t in (np.cos(ang), np.sin(ang)):
        hi, lo = split_bf16(t)
        out.append(np.concatenate([hi, hi, lo], axis=0))
    return np.stack(out)


def twiddles():
    t = np.arange(WIN // BLK)[:, None] * BLK + 255.5
    ang = 2 * np.pi * t * (np.arange(NFREQ)[None, :] + K_LO) / (2 * WIN)
    return np.stack([np.cos(ang), np.sin(ang)], axis=1).astype(np.float32)


def tap_spread():
    j, a, l = np.ogrid[0:TAPS, 0:8, 0:128]
    fwd = (l < 10) & (a - 4 * l + 31 == j)
    rev = (l < 10) & (a - 4 * (9 - l) + 31 == j)
    return np.stack([fwd, rev], axis=1).reshape(TAPS, 4, 512).transpose(1, 0, 2).reshape(4 * TAPS, 512)


def tables():
    tw = twiddles().reshape(16, NFREQ).astype(np.float64)
    hi, rest = split_bf16(tw)
    mid, lo = split_bf16(tw - hi.astype(np.float64))
    rows = np.zeros((TABLE_ROWS, NFREQ), ml_dtypes.bfloat16)
    rows[0:1536] = dft_tables().reshape(1536, NFREQ)
    rows[1536:1792, 0:256] = band_ones()
    rows[1792:1920] = tap_spread()
    rows[1920:1968] = np.concatenate([hi, mid, lo])
    return rows


def lag_table():
    k = np.arange(NFREQ)[:, None] + K_LO
    i = np.arange(LAGS)[None, :] - LAGS // 2 + 2 * WIN
    ang = 2 * np.pi * ((k * i) % (2 * WIN)) / (2 * WIN)
    t = np.stack([np.cos(ang), -np.sin(ang)]) / math.sqrt(NFREQ * NW)
    t = t.reshape(2, 2, 16, 16, LAGS).transpose(1, 2, 0, 3, 4)
    return t.reshape(2 * NFREQ, LAGS).astype(ml_dtypes.bfloat16)


def band_ones():
    g = np.arange(256) // BANDW
    return (g[:, None] == g[None, :]).astype(ml_dtypes.bfloat16)


def dotf(a, b):
    return jnp.dot(a, b, preferred_element_type=F32)


def tdot(a, b):
    return lax.dot_general(a, b, (((0,), (0,)), ((), ())), preferred_element_type=F32)


def hilo(v):
    hi = v.astype(BF)
    return hi, (v - hi.astype(F32)).astype(BF)


def band_rows(unit, start, lane_tile):
    lane = lax.broadcasted_iota(jnp.int32, (8, 128), 1) + 128 * lane_tile
    lo, hi = 128 * lane_tile, 128 * lane_tile + 127
    if start > hi or start + 9 < lo:
        return jnp.zeros((8, 128), F32)
    moved = pltpu.roll(unit, start % 128, 1) if start % 128 else unit
    return jnp.where((lane >= start) & (lane < start + 10), moved, 0.0)


def build_bands(taps, spread, bands):
    row = jnp.concatenate([dotf(taps, spread[TAPS * n:TAPS * n + TAPS]) for n in range(4)], axis=1)
    for v in range(2):
        unit = jnp.concatenate([row[0:1, (8 * v + a) * 128:(8 * v + a + 1) * 128] for a in range(8)], axis=0)
        for r in range(0, 144, 2):
            starts = [(2 * q - 32) if v == 0 else (278 - 2 * q) for q in (r, r + 1)]
            for t in range(2):
                rows = jnp.concatenate([band_rows(unit, s, t) for s in starts], axis=0)
                bands[v, 8 * r:8 * r + 16, 128 * t:128 * t + 128] = rows.astype(BF)


def swap_blocks(vs):
    lane = lax.broadcasted_iota(jnp.int32, vs[0].shape, 1) // 16
    for bit in (1, 2, 4):
        low = lane & bit == 0
        out = list(vs)
        for i in range(8):
            if i & bit == 0:
                a, b = vs[i], vs[i + bit]
                out[i] = jnp.where(low, a, pltpu.roll(b, 16 * bit, 1))
                out[i + bit] = jnp.where(low, pltpu.roll(a, 128 - 16 * bit, 1), b)
        vs = out
    return vs


def build_left(w, l_buf, u, left):
    odd = (lax.broadcasted_iota(jnp.int32, (16, 128), 1) // 16) % 2 == 1
    for q in range(2):
        for g in range(2):
            vs = []
            for i in range(8):
                m, p = 4 * g + i // 2, i % 2
                vs.append(l_buf[w, m, :, 256 * p + 128 * q:256 * p + 128 * q + 128].astype(F32))
            for j, v in enumerate(swap_blocks(vs)):
                turned = jnp.where(odd, pltpu.roll(v, 16, 1), -pltpu.roll(v, 112, 1))
                u[0, 8 * q + j, :, 128 * g:128 * g + 128] = v
                u[1, 8 * q + j, :, 128 * g:128 * g + 128] = turned
    diag = lax.broadcasted_iota(jnp.int32, (16, 256), 1) % 16 == lax.broadcasted_iota(jnp.int32, (16, 256), 0)

    def expand(j, carry):
        for c in range(16):
            for p in range(2):
                row = jnp.broadcast_to(u[p, j, c:c + 1, :], (16, 256))
                r0 = (2 * c + p) * 16
                left[j, r0:r0 + 16, 256 * w:256 * w + 256] = jnp.where(diag, row, 0.0).astype(BF)
        return carry

    lax.fori_loop(0, 16, expand, 0)


def filter_window(x, bands, lhs, dcat):
    rows = 64
    for b in range(16):
        r0 = (b // 2) * rows
        if b == 0:
            lhs[0, 0:rows, 0:128] = jnp.zeros((rows, 128), BF)
            lhs[0, 0:rows, 128:1152] = x[:, 0:1024]
        else:
            lhs[b % 2, r0:r0 + rows, :] = x[:, 1024 * b - 128:1024 * b + 1024]
    even = dotf(lhs[0], bands[0])
    odd = dotf(lhs[1], bands[1])
    for i, v in enumerate((even + odd, even - odd)):
        hi, lo = hilo(v)
        dcat[i, :, 0:256] = hi
        dcat[i, :, 256:512] = lo
        dcat[i, :, 512:768] = hi


def spectrum_half(h, dcat, tab, tw, ones, sel, wst, picks):
    rows = 64
    cols = slice(256 * h, 256 * h + 256)
    yc = dotf(dcat[0], tab[0:768, cols])
    ys = dotf(dcat[1], tab[768:1536, cols])
    xre = xim = 0.0
    for b in range(WIN // BLK):
        c = tw[2 * b:2 * b + 1, cols]
        s = tw[2 * b + 1:2 * b + 2, cols]
        bc = yc[b * rows:(b + 1) * rows]
        bs = ys[b * rows:(b + 1) * rows]
        xre = xre + (bc * c - bs * s)
        xim = xim - (bs * c + bc * s)
    phi, plo = hilo(xre * xre + xim * xim)
    power = dotf(phi, ones) + dotf(plo, ones)
    scale = lax.rsqrt(power * (1.0 / BANDW) + 1e-6)
    wre = (xre * scale).astype(BF)
    wim = (xim * scale).astype(BF)
    for z in range(4):
        wst[h, z, :, 0:256] = wre[16 * z:16 * z + 16]
        wst[h, z, :, 256:512] = wim[16 * z:16 * z + 16]
    for p, part in enumerate((wre, wim)):
        picked = tdot(part, sel).astype(BF)
        for j in range(16):
            picks[h, j // 4, j % 4, p] = picked[16 * j:16 * j + 16]


def cross_kernel(x_hbm, rows_hbm, small, xf_ref, x_buf, tab, aux, tw, bands, lhs, dcat, picks, wst, r1, acc, r2, red, zin, s_buf, l_buf, u, left, part, xs,
                 in_sem, p_send, p_recv, z_send, z_recv, t_send, t_recv, l_send, l_recv, l_own, g_send, g_recv,
                 x_sem):
    m = lax.axis_index("tm")
    ch = lax.axis_index("chan")
    core = m % 2
    zl = m // 2
    zh, xy = ch // 16, ch % 16
    x, y = xy // 4, xy % 4
    z = zh * 4 + zl
    barrier = pltpu.get_barrier_semaphore()
    loads = [pltpu.make_async_copy(rows_hbm.at[pl.ds(0, 1536)], tab, in_sem.at[3])]
    loads += [pltpu.make_async_copy(x_hbm.at[w], x_buf.at[w], in_sem.at[w]) for w in range(3)]
    aux_load = pltpu.make_async_copy(rows_hbm.at[pl.ds(1536, 432)], aux, in_sem.at[4])
    for c in [aux_load, loads[1], loads[0]] + loads[2:]:
        c.start()

    def xy_peer(dx, dy):
        return ((x + dx) % 4) * 4 + (y + dy) % 4

    def along(axis, d):
        return (m, zh * 16 + (xy_peer(d, 0) if axis == 0 else xy_peer(0, d)))

    def on_ring(d, to_core):
        zz = (z + d) % 8
        return ((zz % 4) * 2 + to_core, (zz // 4) * 16 + xy)

    for axis in range(2):
        for d in (1, 2, 3):
            pl.semaphore_signal(barrier, inc=1, device_id=along(axis, d), device_id_type=MESH)
    for d in range(8):
        for flip in range(2):
            if d or flip:
                pl.semaphore_signal(barrier, inc=1, device_id=on_ring(d, (core + flip) % 2), device_id_type=MESH)

    def remote(src, dst, ssem, rsem, dev):
        pltpu.make_async_remote_copy(src_ref=src, dst_ref=dst, send_sem=ssem, recv_sem=rsem,
                                     device_id=dev, device_id_type=MESH).start()

    def take(ref, sem):
        pltpu.make_async_copy(ref, ref, sem).wait()

    aux_load.wait()
    ids = (ch * 64 + lax.broadcasted_iota(jnp.int32, (64, SRC), 0)).astype(F32)
    sel = jnp.maximum(1.0 - jnp.abs(ids - small[1:2, :]), 0.0).astype(BF)
    tw[...] = aux[384:400].astype(F32) + aux[400:416].astype(F32) + aux[416:432].astype(F32)
    ones = aux[0:256, 0:256]
    build_bands(small[0:1, 0:TAPS].astype(BF), aux[256:384], bands)
    mine = (x, y)
    arrived = {}

    def mark(w, *keys):
        ready = []
        for a, b in keys:
            for f in range(2):
                key = (a, b) if f == 0 else (b, a)
                arrived[w, key] = arrived.get((w, key), 0) + 1
                if arrived[w, key] == 2:
                    ready.append(xy_peer(*key))
        if w == 1:
            for j in ready:
                part[j] = dotf(left[j, :, 0:512], s_buf[j, 0:2].reshape(512, SRC))
        if w == 2:
            for j in ready:
                o = part[j] + dotf(left[j, :, 512:768], s_buf[j, 2].reshape(256, SRC))
                xs[:, j] = o.astype(BF).reshape(2, 16, 16, SRC)
            for j in ready:
                remote(xs.at[1 - core, j], xf_ref.at[core, j], x_sem.at[0], x_sem.at[1], (m + 1 - 2 * core, ch))
                pltpu.make_async_copy(xs.at[core, j], xf_ref.at[core, j], x_sem.at[2]).start()

    def chain(w):
        def chunk(f, d):
            return picks.at[w, 0, (x + d) % 4] if f == 0 else picks.at[w, 1, :, (y + d) % 4]

        for d in (2, 1, 3):
            for f in range(2):
                remote(chunk(f, d), r1.at[w, f, d - 1], p_send.at[w, 0], p_recv.at[w, 0, f], along(f, d))
        for o in range(1, 8):
            mm = (m + o) % 8
            remote(wst.at[w, mm % 2, mm // 2], l_buf.at[w, m], l_send.at[w], l_recv.at[w], (mm, ch))
        pltpu.make_async_copy(wst.at[w, core, zl], l_buf.at[w, m], l_own.at[w]).start()
        yield
        for f in range(2):
            take(r1.at[w, f], p_recv.at[w, 0, f])
            acc[w, f] = chunk(f, 0)[...] + r1[w, f, 0] + r1[w, f, 1] + r1[w, f, 2]
            for d in (2, 1, 3):
                remote(acc.at[w, f, (mine[1 - f] + d) % 4], r2.at[w, f, d - 1], p_send.at[w, 1],
                       p_recv.at[w, 1, f], along(1 - f, d))
        yield
        for f in range(2):
            take(r2.at[w, f], p_recv.at[w, 1, f])
            red[w, 0, f] = acc[w, f, mine[1 - f]] + r2[w, f, 0] + r2[w, f, 1] + r2[w, f, 2]
        remote(red.at[w, 0], zin.at[w], z_send.at[w], z_recv.at[w], on_ring(4, core))
        yield
        take(zin.at[w], z_recv.at[w])
        red[w, 1] = red[w, 0] + zin[w]
        for d in (2 - 4 * core, 1, -1):
            for flip in range(2):
                to = (core + flip) % 2
                remote(red.at[w, 1, to], s_buf.at[xy, w, m], t_send.at[w], t_recv.at[w], on_ring(d + 8, to))
        remote(red.at[w, 1, 1 - core], s_buf.at[xy, w, m], t_send.at[w], t_recv.at[w], on_ring(0, 1 - core))
        s_buf[xy, w, m] = red[w, 1, core]
        yield
        take(s_buf.at[xy, w, pl.ds(0, 7)], t_recv.at[w])

        def send(f, a, b, slot, d, axis):
            src = xy_peer(a, b) if f == 0 else xy_peer(b, a)
            part = s_buf.at[src, w, pl.ds(4 * f, 4)]
            remote(part, part, g_send.at[w], g_recv.at[w, slot], along(axis, d))

        def second(f, a, slot):
            send(f, a, 0, slot, 1, 1 - f)
            send(f, a, 0, slot, 3, 1 - f)

        def forward(f, a, slot):
            first = 1 if a % 2 == 0 else 3
            send(f, a, 4 - first, slot, first, 1 - f)

        def got(shards, slot):
            take(s_buf.at[pl.ds(0, shards), w], g_recv.at[w, slot])

        for f in range(2):
            send(f, 0, 0, 0, 1, f)
            send(f, 0, 0, 0, 3, f)
        for f in range(2):
            second(f, 0, 2)
        mark(w, (0, 0))
        yield
        got(2, 0)
        for f in range(2):
            first = 1 if f == 0 else 3
            send(f, 4 - first, 0, 1, first, f)
        for f in range(2):
            second(f, 3, 4)
            second(f, 1, 4)
        got(2, 2)
        for f in range(2):
            forward(f, 0, 3)
        mark(w, (1, 0), (0, 1), (3, 0), (0, 3))
        yield
        got(1, 1)
        for f in range(2):
            second(f, 2, 6)
        got(4, 4)
        for a in (3, 1):
            for f in range(2):
                forward(f, a, 5)
        mark(w, (2, 0), (1, 1), (1, 3), (3, 1), (3, 3))
        yield
        got(2, 6)
        for f in range(2):
            forward(f, 2, 7)
        got(1, 3)
        got(2, 5)
        mark(w, (0, 2), (2, 1), (1, 2), (2, 3), (3, 2))
        yield
        got(1, 7)
        mark(w, (2, 2))
        yield

    def filt(w):
        loads[1 + w].wait()
        filter_window(x_buf.at[w], bands, lhs, dcat)

    def half(w, h):
        spectrum_half(h, dcat, tab, tw, ones, sel, wst.at[w], picks.at[w])

    def build(w):
        take(l_buf.at[w, m], l_own.at[w])
        take(l_buf.at[w, pl.ds(0, 7)], l_recv.at[w])
        build_left(w, l_buf, u, left)

    chains = [chain(w) for w in range(3)]

    def go(*ws):
        for w in ws:
            next(chains[w])

    filt(0)
    loads[0].wait()
    half(0, 0)
    half(0, 1)
    pl.semaphore_wait(barrier, 21)
    go(0)
    filt(1)
    half(1, 0)
    half(1, 1)
    go(0, 1)
    filt(2)
    half(2, 0)
    half(2, 1)
    go(0, 2, 1, 2, 1, 0, 2, 0)
    build(0)
    go(1)
    build(1)
    go(0)
    build(2)
    go(1, 2, 0, 2, 1, 2, 1, 0, 2, 1, 2, 0, 1, 2)
    for w in range(3):
        take(r1.at[w], p_send.at[w, 0])
        take(r2.at[w], p_send.at[w, 1])
        take(l_buf.at[w, pl.ds(0, 7)], l_send.at[w])
        take(zin.at[w], z_send.at[w])
        take(s_buf.at[xy, w, pl.ds(0, 7)], t_send.at[w])
        take(s_buf.at[pl.ds(0, 15), w], g_send.at[w])
    for n in range(3):
        take(xs.at[0], x_sem.at[n])


def cross(x, small):
    hbm = pl.BlockSpec(memory_space=pltpu.HBM)
    dma = pltpu.SemaphoreType.DMA
    tile = (2, 16, SRC)
    return pl.pallas_call(
        cross_kernel,
        in_specs=[hbm, hbm, pl.BlockSpec(memory_space=pltpu.VMEM)],
        out_specs=pl.BlockSpec(memory_space=pl.ANY),
        out_shape=jax.ShapeDtypeStruct((2, 16, 16, 16, SRC), BF),
        scratch_shapes=[
            pltpu.VMEM((3, 64, 4 * WIN), BF),
            pltpu.VMEM((1536, NFREQ), BF),
            pltpu.VMEM((432, NFREQ), BF),
            pltpu.VMEM((16, NFREQ), F32),
            pltpu.VMEM((2, 1152, 256), BF),
            pltpu.VMEM((2, 512, 1152), BF),
            pltpu.VMEM((2, 512, 768), BF),
            pltpu.VMEM((3, 2, 4, 4) + tile, BF),
            pltpu.VMEM((3, 2, 4, 16, 512), BF),
            pltpu.VMEM((3, 2, 3, 4) + tile, BF),
            pltpu.VMEM((3, 2, 4) + tile, BF),
            pltpu.VMEM((3, 2, 3) + tile, BF),
            pltpu.VMEM((3, 2, 2) + tile, BF),
            pltpu.VMEM((3, 2) + tile, BF),
            pltpu.VMEM((16, 3, 8) + tile, BF),
            pltpu.VMEM((3, 8, 16, 512), BF),
            pltpu.VMEM((2, 16, 16, 256), F32),
            pltpu.VMEM((16, 512, 768), BF),
            pltpu.VMEM((16, 512, SRC), F32),
            pltpu.VMEM((2, 16, 16, 16, SRC), BF),
            dma((5,)), dma((3, 2)), dma((3, 2, 2)), dma((3,)), dma((3,)), dma((3,)), dma((3,)), dma((3,)), dma((3,)),
            dma((3,)), dma((3,)), dma((3, 8)), dma((3,)),
        ],
        compiler_params=pltpu.CompilerParams(collective_id=0, has_side_effects=True, vmem_limit_bytes=50 << 20),
        name="cross",
    )(x, jnp.asarray(tables()), small)


def lags_kernel(xf_ref, lt_ref, out_hbm, lhs, blocks, sems):
    for c in range(8):
        lhs[c * SRC:(c + 1) * SRC, :] = xf_ref[:, :, 2 * c:2 * c + 2].reshape(1024, SRC).T
    writes = []
    for n in range(4):
        cols = pl.ds(256 * n, 256)
        o = dotf(lhs[...], lt_ref[:, cols])
        for c in range(8):
            blocks[n, :, c, :] = o[c * SRC:(c + 1) * SRC]
        writes.append(pltpu.make_async_copy(blocks.at[n], out_hbm.at[:, :, cols], sems.at[n]))
        writes[n].start()
    for w in writes:
        w.wait()


def lags(xf):
    vm = pl.BlockSpec(memory_space=pltpu.VMEM)
    return pl.pallas_call(
        lags_kernel,
        in_specs=[vm, vm],
        out_specs=pl.BlockSpec(memory_space=pltpu.HBM),
        out_shape=jax.ShapeDtypeStruct((SRC, 8, LAGS), F32),
        scratch_shapes=[
            pltpu.VMEM((1024, 1024), BF),
            pltpu.VMEM((4, SRC, 8, 256), F32),
            pltpu.SemaphoreType.DMA((4,)),
        ],
        compiler_params=pltpu.CompilerParams(vmem_limit_bytes=24 << 20),
        name="lags",
    )(xf, jnp.asarray(lag_table()))


def on_device(strain_rate, fir_taps, source_channels):
    x = jnp.transpose(strain_rate, (1, 0, 2))
    taps = jnp.pad(fir_taps.astype(F32), (0, SRC - TAPS))
    first = lax.broadcasted_iota(jnp.int32, (2, SRC), 0) == 0
    xf = cross(x, jnp.where(first, taps[None, :], source_channels.astype(F32)[None, :]))
    return lags(xf)


def solution(mesh):
    placed = (P("chan", "tm", None), P(), P())
    return jax.shard_map(
        on_device,
        mesh=mesh,
        in_specs=placed,
        out_specs=P(None, ("chan", "tm"), None),
        check_vma=False,
    )
```

```python
import functools
import math

import jax
import jax.numpy as jnp
import ml_dtypes
import numpy as np
from jax import lax
from jax.experimental import pallas as pl
from jax.experimental.pallas import tpu as pltpu
from jax.sharding import PartitionSpec as P

WIN = 4096
NFREQ = 512
BANDW = 64
K_LO = 32
LAGS = 1024
TAPS = 32
NW = 24
SRC = 128
BLK = 512
TABLE_ROWS = 10240
BF = jnp.bfloat16
F32 = jnp.float32
MESH = pl.DeviceIdType.MESH
VLIM = 56 * 1024 * 1024


def split_bf16(a):
    hi = a.astype(ml_dtypes.bfloat16)
    lo = (a - hi.astype(np.float64)).astype(ml_dtypes.bfloat16)
    return hi, lo


def dft_tables():
    u = np.arange(256)[:, None] - 255.5
    ang = 2 * np.pi * u * (np.arange(NFREQ)[None, :] + K_LO) / (2 * WIN)
    out = []
    for t in (np.cos(ang), np.sin(ang)):
        hi, lo = split_bf16(t)
        out.append(np.concatenate([hi, hi, lo], axis=0))
    return np.stack(out)


def twiddles():
    t = np.arange(WIN // BLK)[:, None] * BLK + 255.5
    ang = 2 * np.pi * t * (np.arange(NFREQ)[None, :] + K_LO) / (2 * WIN)
    return np.stack([np.cos(ang), np.sin(ang)], axis=1).astype(np.float32)


def tap_spread():
    j, a, l = np.ogrid[0:TAPS, 0:8, 0:128]
    fwd = (l < 10) & (a - 4 * l + 31 == j)
    rev = (l < 10) & (a - 4 * (9 - l) + 31 == j)
    return np.stack([fwd, rev], axis=1).reshape(TAPS, 4, 512).transpose(1, 0, 2).reshape(4 * TAPS, 512)


def tables():
    tw = twiddles().reshape(16, NFREQ).astype(np.float64)
    hi, rest = split_bf16(tw)
    mid, lo = split_bf16(tw - hi.astype(np.float64))
    rows = np.zeros((TABLE_ROWS, NFREQ), ml_dtypes.bfloat16)
    rows[0:1536] = dft_tables().reshape(1536, NFREQ)
    rows[1536:1792, 0:256] = band_ones()
    rows[1792:1920] = tap_spread()
    rows[1920:1968] = np.concatenate([hi, mid, lo])
    return rows


def lag_table():
    k = np.arange(NFREQ)[:, None] + K_LO
    i = np.arange(LAGS)[None, :] - LAGS // 2 + 2 * WIN
    ang = 2 * np.pi * ((k * i) % (2 * WIN)) / (2 * WIN)
    t = np.stack([np.cos(ang), -np.sin(ang)]) / math.sqrt(NFREQ * NW)
    t = t.reshape(2, 2, 16, 16, LAGS).transpose(1, 2, 0, 3, 4)
    return t.reshape(2 * NFREQ, LAGS).astype(ml_dtypes.bfloat16)


def band_ones():
    g = np.arange(256) // BANDW
    return (g[:, None] == g[None, :]).astype(ml_dtypes.bfloat16)


def dotf(a, b):
    return jnp.dot(a, b, preferred_element_type=F32)


def tdot(a, b):
    return lax.dot_general(a, b, (((0,), (0,)), ((), ())), preferred_element_type=F32)


def hilo(v):
    hi = v.astype(BF)
    return hi, (v - hi.astype(F32)).astype(BF)


def band_rows(unit, start, lane_tile):
    lane = lax.broadcasted_iota(jnp.int32, (8, 128), 1) + 128 * lane_tile
    lo, hi = 128 * lane_tile, 128 * lane_tile + 127
    if start > hi or start + 9 < lo:
        return jnp.zeros((8, 128), F32)
    moved = pltpu.roll(unit, start % 128, 1) if start % 128 else unit
    return jnp.where((lane >= start) & (lane < start + 10), moved, 0.0)


def build_bands(taps, spread, bands):
    row = jnp.concatenate([dotf(taps, spread[TAPS * n:TAPS * n + TAPS]) for n in range(4)], axis=1)
    for v in range(2):
        unit = jnp.concatenate([row[0:1, (8 * v + a) * 128:(8 * v + a + 1) * 128] for a in range(8)], axis=0)
        for r in range(0, 144, 2):
            starts = [(2 * q - 32) if v == 0 else (278 - 2 * q) for q in (r, r + 1)]
            for t in range(2):
                rows = jnp.concatenate([band_rows(unit, s, t) for s in starts], axis=0)
                bands[v, 8 * r:8 * r + 16, 128 * t:128 * t + 128] = rows.astype(BF)


def swap_blocks(vs):
    lane = lax.broadcasted_iota(jnp.int32, vs[0].shape, 1) // 16
    for bit in (1, 2, 4):
        low = lane & bit == 0
        out = list(vs)
        for i in range(8):
            if i & bit == 0:
                a, b = vs[i], vs[i + bit]
                out[i] = jnp.where(low, a, pltpu.roll(b, 16 * bit, 1))
                out[i + bit] = jnp.where(low, pltpu.roll(a, 128 - 16 * bit, 1), b)
        vs = out
    return vs


def build_left(w, l_buf, u, left):
    odd = (lax.broadcasted_iota(jnp.int32, (16, 128), 1) // 16) % 2 == 1
    for q in range(2):
        for g in range(2):
            vs = []
            for i in range(8):
                m, p = 4 * g + i // 2, i % 2
                vs.append(l_buf[w, m, :, 256 * p + 128 * q:256 * p + 128 * q + 128].astype(F32))
            for j, v in enumerate(swap_blocks(vs)):
                turned = jnp.where(odd, pltpu.roll(v, 16, 1), -pltpu.roll(v, 112, 1))
                u[0, 8 * q + j, :, 128 * g:128 * g + 128] = v
                u[1, 8 * q + j, :, 128 * g:128 * g + 128] = turned
    diag = lax.broadcasted_iota(jnp.int32, (16, 256), 1) % 16 == lax.broadcasted_iota(jnp.int32, (16, 256), 0)

    def expand(j, carry):
        for c in range(16):
            for p in range(2):
                row = jnp.broadcast_to(u[p, j, c:c + 1, :], (16, 256))
                r0 = (2 * c + p) * 16
                left[j, r0:r0 + 16, 256 * w:256 * w + 256] = jnp.where(diag, row, 0.0).astype(BF)
        return carry

    lax.fori_loop(0, 16, expand, 0)


def filter_window(x, bands, lhs, dcat):
    rows = 64
    for b in range(16):
        r0 = (b // 2) * rows
        if b == 0:
            lhs[0, 0:rows, 0:128] = jnp.zeros((rows, 128), BF)
            lhs[0, 0:rows, 128:1152] = x[:, 0:1024]
        else:
            lhs[b % 2, r0:r0 + rows, :] = x[:, 1024 * b - 128:1024 * b + 1024]
    even = dotf(lhs[0], bands[0])
    odd = dotf(lhs[1], bands[1])
    for i, v in enumerate((even + odd, even - odd)):
        hi, lo = hilo(v)
        dcat[i, :, 0:256] = hi
        dcat[i, :, 256:512] = lo
        dcat[i, :, 512:768] = hi


def spectrum_half(h, dcat, tab, tw, ones, sel, wst, picks):
    rows = 64
    cols = slice(256 * h, 256 * h + 256)
    yc = dotf(dcat[0], tab[0:768, cols])
    ys = dotf(dcat[1], tab[768:1536, cols])
    xre = xim = 0.0
    for b in range(WIN // BLK):
        c = tw[2 * b:2 * b + 1, cols]
        s = tw[2 * b + 1:2 * b + 2, cols]
        bc = yc[b * rows:(b + 1) * rows]
        bs = ys[b * rows:(b + 1) * rows]
        xre = xre + (bc * c - bs * s)
        xim = xim - (bs * c + bc * s)
    phi, plo = hilo(xre * xre + xim * xim)
    power = dotf(phi, ones) + dotf(plo, ones)
    scale = lax.rsqrt(power * (1.0 / BANDW) + 1e-6)
    wre = (xre * scale).astype(BF)
    wim = (xim * scale).astype(BF)
    for z in range(4):
        wst[h, z, :, 0:256] = wre[16 * z:16 * z + 16]
        wst[h, z, :, 256:512] = wim[16 * z:16 * z + 16]
    for p, part in enumerate((wre, wim)):
        picked = tdot(part, sel).astype(BF)
        for j in range(16):
            picks[h, j // 4, j % 4, p] = picked[16 * j:16 * j + 16]


def cross_kernel(x_hbm, rows_hbm, small, xf_ref, x_buf, tab, aux, tw, bands, lhs, dcat, picks, wst, r1, acc, r2, red, zin, s_buf, l_buf, u, left, part, xs,
                 in_sem, p_send, p_recv, z_send, z_recv, t_send, t_recv, l_send, l_recv, l_own, g_send, g_recv,
                 x_sem):
    m = lax.axis_index("tm")
    ch = lax.axis_index("chan")
    core = m % 2
    zl = m // 2
    zh, xy = ch // 16, ch % 16
    x, y = xy // 4, xy % 4
    z = zh * 4 + zl
    barrier = pltpu.get_barrier_semaphore()
    loads = [pltpu.make_async_copy(rows_hbm.at[pl.ds(0, 1536)], tab, in_sem.at[3])]
    loads += [pltpu.make_async_copy(x_hbm.at[w], x_buf.at[w], in_sem.at[w]) for w in range(3)]
    aux_load = pltpu.make_async_copy(rows_hbm.at[pl.ds(1536, 432)], aux, in_sem.at[4])
    for c in [aux_load, loads[1], loads[0]] + loads[2:]:
        c.start()

    def xy_peer(dx, dy):
        return ((x + dx) % 4) * 4 + (y + dy) % 4

    def along(axis, d):
        return (m, zh * 16 + (xy_peer(d, 0) if axis == 0 else xy_peer(0, d)))

    def on_ring(d, to_core):
        zz = (z + d) % 8
        return ((zz % 4) * 2 + to_core, (zz // 4) * 16 + xy)

    for axis in range(2):
        for d in (1, 2, 3):
            pl.semaphore_signal(barrier, inc=1, device_id=along(axis, d), device_id_type=MESH)
    for d in range(8):
        for flip in range(2):
            if d or flip:
                pl.semaphore_signal(barrier, inc=1, device_id=on_ring(d, (core + flip) % 2), device_id_type=MESH)

    def remote(src, dst, ssem, rsem, dev):
        pltpu.make_async_remote_copy(src_ref=src, dst_ref=dst, send_sem=ssem, recv_sem=rsem,
                                     device_id=dev, device_id_type=MESH).start()

    def take(ref, sem):
        pltpu.make_async_copy(ref, ref, sem).wait()

    aux_load.wait()
    ids = (ch * 64 + lax.broadcasted_iota(jnp.int32, (64, SRC), 0)).astype(F32)
    sel = jnp.maximum(1.0 - jnp.abs(ids - small[1:2, :]), 0.0).astype(BF)
    tw[...] = aux[384:400].astype(F32) + aux[400:416].astype(F32) + aux[416:432].astype(F32)
    ones = aux[0:256, 0:256]
    build_bands(small[0:1, 0:TAPS].astype(BF), aux[256:384], bands)
    mine = (x, y)
    arrived = {}

    def mark(w, *keys):
        ready = []
        for a, b in keys:
            for f in range(2):
                key = (a, b) if f == 0 else (b, a)
                arrived[w, key] = arrived.get((w, key), 0) + 1
                if arrived[w, key] == 2:
                    ready.append(xy_peer(*key))
        if w == 1:
            for j in ready:
                part[j] = dotf(left[j, :, 0:512], s_buf[j, 0:2].reshape(512, SRC))
        if w == 2:
            for j in ready:
                o = part[j] + dotf(left[j, :, 512:768], s_buf[j, 2].reshape(256, SRC))
                xs[:, j] = o.astype(BF).reshape(2, 16, 16, SRC)
            for j in ready:
                remote(xs.at[1 - core, j], xf_ref.at[core, j], x_sem.at[0], x_sem.at[1], (m + 1 - 2 * core, ch))
                pltpu.make_async_copy(xs.at[core, j], xf_ref.at[core, j], x_sem.at[2]).start()

    def chain(w):
        def chunk(f, d):
            return picks.at[w, 0, (x + d) % 4] if f == 0 else picks.at[w, 1, :, (y + d) % 4]

        for d in (2, 1, 3):
            for f in range(2):
                remote(chunk(f, d), r1.at[w, f, d - 1], p_send.at[w, 0], p_recv.at[w, 0, f], along(f, d))
        for o in range(1, 8):
            mm = (m + o) % 8
            remote(wst.at[w, mm % 2, mm // 2], l_buf.at[w, m], l_send.at[w], l_recv.at[w], (mm, ch))
        pltpu.make_async_copy(wst.at[w, core, zl], l_buf.at[w, m], l_own.at[w]).start()
        yield
        for f in range(2):
            take(r1.at[w, f], p_recv.at[w, 0, f])
            acc[w, f] = chunk(f, 0)[...] + r1[w, f, 0] + r1[w, f, 1] + r1[w, f, 2]
            for d in (2, 1, 3):
                remote(acc.at[w, f, (mine[1 - f] + d) % 4], r2.at[w, f, d - 1], p_send.at[w, 1],
                       p_recv.at[w, 1, f], along(1 - f, d))
        yield
        for f in range(2):
            take(r2.at[w, f], p_recv.at[w, 1, f])
            red[w, 0, f] = acc[w, f, mine[1 - f]] + r2[w, f, 0] + r2[w, f, 1] + r2[w, f, 2]
        remote(red.at[w, 0], zin.at[w], z_send.at[w], z_recv.at[w], on_ring(4, core))
        yield
        take(zin.at[w], z_recv.at[w])
        red[w, 1] = red[w, 0] + zin[w]
        for d in (2 - 4 * core, 1, -1):
            for flip in range(2):
                to = (core + flip) % 2
                remote(red.at[w, 1, to], s_buf.at[xy, w, m], t_send.at[w], t_recv.at[w], on_ring(d + 8, to))
        remote(red.at[w, 1, 1 - core], s_buf.at[xy, w, m], t_send.at[w], t_recv.at[w], on_ring(0, 1 - core))
        s_buf[xy, w, m] = red[w, 1, core]
        yield
        take(s_buf.at[xy, w, pl.ds(0, 7)], t_recv.at[w])

        def send(f, a, b, slot, d, axis):
            src = xy_peer(a, b) if f == 0 else xy_peer(b, a)
            part = s_buf.at[src, w, pl.ds(4 * f, 4)]
            remote(part, part, g_send.at[w], g_recv.at[w, slot], along(axis, d))

        def second(f, a, slot):
            send(f, a, 0, slot, 1, 1 - f)
            send(f, a, 0, slot, 3, 1 - f)

        def forward(f, a, slot):
            first = 1 if a % 2 == 0 else 3
            send(f, a, 4 - first, slot, first, 1 - f)

        def got(shards, slot):
            take(s_buf.at[pl.ds(0, shards), w], g_recv.at[w, slot])

        for f in range(2):
            send(f, 0, 0, 0, 1, f)
            send(f, 0, 0, 0, 3, f)
        for f in range(2):
            second(f, 0, 2)
        mark(w, (0, 0))
        yield
        got(2, 0)
        for f in range(2):
            first = 1 if (f + w) % 2 == 0 else 3
            send(f, 4 - first, 0, 1, first, f)
        for f in range(2):
            second(f, 3, 4)
            second(f, 1, 4)
        got(2, 2)
        for f in range(2):
            forward(f, 0, 3)
        mark(w, (1, 0), (0, 1), (3, 0), (0, 3))
        yield
        got(1, 1)
        for f in range(2):
            second(f, 2, 6)
        got(4, 4)
        for a in (3, 1):
            for f in range(2):
                forward(f, a, 5)
        mark(w, (2, 0), (1, 1), (1, 3), (3, 1), (3, 3))
        yield
        got(2, 6)
        for f in range(2):
            forward(f, 2, 7)
        got(1, 3)
        got(2, 5)
        mark(w, (0, 2), (2, 1), (1, 2), (2, 3), (3, 2))
        yield
        got(1, 7)
        mark(w, (2, 2))
        yield

    def filt(w):
        loads[1 + w].wait()
        filter_window(x_buf.at[w], bands, lhs, dcat)

    def half(w, h):
        spectrum_half(h, dcat, tab, tw, ones, sel, wst.at[w], picks.at[w])

    def build(w):
        take(l_buf.at[w, m], l_own.at[w])
        take(l_buf.at[w, pl.ds(0, 7)], l_recv.at[w])
        build_left(w, l_buf, u, left)

    chains = [chain(w) for w in range(3)]

    def go(*ws):
        for w in ws:
            next(chains[w])

    filt(0)
    loads[0].wait()
    half(0, 0)
    half(0, 1)
    pl.semaphore_wait(barrier, 21)
    go(0)
    filt(1)
    half(1, 0)
    half(1, 1)
    go(0, 1)
    filt(2)
    half(2, 0)
    half(2, 1)
    go(0, 2, 1, 2, 1, 0, 2, 0)
    build(0)
    go(1)
    build(1)
    go(0)
    build(2)
    go(1, 2, 0, 2, 1, 2, 1, 0, 2, 1, 2, 0, 1, 2)
    for w in range(3):
        take(r1.at[w], p_send.at[w, 0])
        take(r2.at[w], p_send.at[w, 1])
        take(l_buf.at[w, pl.ds(0, 7)], l_send.at[w])
        take(zin.at[w], z_send.at[w])
        take(s_buf.at[xy, w, pl.ds(0, 7)], t_send.at[w])
        take(s_buf.at[pl.ds(0, 15), w], g_send.at[w])
    for n in range(3):
        take(xs.at[0], x_sem.at[n])


def cross(x, small):
    hbm = pl.BlockSpec(memory_space=pltpu.HBM)
    dma = pltpu.SemaphoreType.DMA
    tile = (2, 16, SRC)
    return pl.pallas_call(
        cross_kernel,
        in_specs=[hbm, hbm, pl.BlockSpec(memory_space=pltpu.VMEM)],
        out_specs=pl.BlockSpec(memory_space=pl.ANY),
        out_shape=jax.ShapeDtypeStruct((2, 16, 16, 16, SRC), BF),
        scratch_shapes=[
            pltpu.VMEM((3, 64, 4 * WIN), BF),
            pltpu.VMEM((1536, NFREQ), BF),
            pltpu.VMEM((432, NFREQ), BF),
            pltpu.VMEM((16, NFREQ), F32),
            pltpu.VMEM((2, 1152, 256), BF),
            pltpu.VMEM((2, 512, 1152), BF),
            pltpu.VMEM((2, 512, 768), BF),
            pltpu.VMEM((3, 2, 4, 4) + tile, BF),
            pltpu.VMEM((3, 2, 4, 16, 512), BF),
            pltpu.VMEM((3, 2, 3, 4) + tile, BF),
            pltpu.VMEM((3, 2, 4) + tile, BF),
            pltpu.VMEM((3, 2, 3) + tile, BF),
            pltpu.VMEM((3, 2, 2) + tile, BF),
            pltpu.VMEM((3, 2) + tile, BF),
            pltpu.VMEM((16, 3, 8) + tile, BF),
            pltpu.VMEM((3, 8, 16, 512), BF),
            pltpu.VMEM((2, 16, 16, 256), F32),
            pltpu.VMEM((16, 512, 768), BF),
            pltpu.VMEM((16, 512, SRC), F32),
            pltpu.VMEM((2, 16, 16, 16, SRC), BF),
            dma((5,)), dma((3, 2)), dma((3, 2, 2)), dma((3,)), dma((3,)), dma((3,)), dma((3,)), dma((3,)), dma((3,)),
            dma((3,)), dma((3,)), dma((3, 8)), dma((3,)),
        ],
        compiler_params=pltpu.CompilerParams(collective_id=0, has_side_effects=True, vmem_limit_bytes=50 << 20),
        name="cross",
    )(x, jnp.asarray(tables()), small)


def lags_kernel(xf_ref, lt_ref, out_hbm, lhs, blocks, sems):
    for c in range(8):
        lhs[c * SRC:(c + 1) * SRC, :] = xf_ref[:, :, 2 * c:2 * c + 2].reshape(1024, SRC).T
    writes = []
    for n in range(4):
        cols = pl.ds(256 * n, 256)
        o = dotf(lhs[...], lt_ref[:, cols])
        for c in range(8):
            blocks[n, :, c, :] = o[c * SRC:(c + 1) * SRC]
        writes.append(pltpu.make_async_copy(blocks.at[n], out_hbm.at[:, :, cols], sems.at[n]))
        writes[n].start()
    for w in writes:
        w.wait()


def lags(xf):
    vm = pl.BlockSpec(memory_space=pltpu.VMEM)
    return pl.pallas_call(
        lags_kernel,
        in_specs=[vm, vm],
        out_specs=pl.BlockSpec(memory_space=pltpu.HBM),
        out_shape=jax.ShapeDtypeStruct((SRC, 8, LAGS), F32),
        scratch_shapes=[
            pltpu.VMEM((1024, 1024), BF),
            pltpu.VMEM((4, SRC, 8, 256), F32),
            pltpu.SemaphoreType.DMA((4,)),
        ],
        compiler_params=pltpu.CompilerParams(vmem_limit_bytes=24 << 20),
        name="lags",
    )(xf, jnp.asarray(lag_table()))


def on_device(strain_rate, fir_taps, source_channels):
    x = jnp.transpose(strain_rate, (1, 0, 2))
    taps = jnp.pad(fir_taps.astype(F32), (0, SRC - TAPS))
    first = lax.broadcasted_iota(jnp.int32, (2, SRC), 0) == 0
    xf = cross(x, jnp.where(first, taps[None, :], source_channels.astype(F32)[None, :]))
    return lags(xf)


def solution(mesh):
    placed = (P("chan", "tm", None), P(), P())
    return jax.shard_map(
        on_device,
        mesh=mesh,
        in_specs=placed,
        out_specs=P(None, ("chan", "tm"), None),
        check_vma=False,
    )
```
